32 devices in a mesh: ctx: 8 (over z, x), head: 4 (over y, core).
Axes of the slice: x: 2, y: 2, z: 4, core: 2. Of those that a mesh axis runs over, the one named last changes fastest.
Arguments:
- x_raw: bfloat16 [2048, 8192], P('ctx', 'head'), may hold values from -6 to 6
- bc_raw: bfloat16 [2048, 256], P('ctx'), may hold values from -6 to 6
- conv_x_w: bfloat16 [4, 8192], P(None, 'head'), may hold values from -3 to 3
- conv_bc_w: bfloat16 [4, 256], replicated, may hold values from -3 to 3
- dt_raw: float32 [128, 2048], P('head', 'ctx'), may hold values from -7 to 0
- a_log: float32 [128], P('head'), may hold values from -10 to 1
- d_skip: float32 [128], P('head'), may hold values from 0.5 to 1.5
- doc_starts: int32 [8], P('ctx'), may hold values from 0 to 256, as said below
- grad_y: bfloat16 [2048, 8192], P('ctx', 'head'), may hold values from -6 to 6
Outputs:
- y_out: bfloat16 [2048, 8192], P('ctx', 'head')
- grad_x_raw: bfloat16 [2048, 8192], P('ctx', 'head')
- grad_bc_raw: bfloat16 [2048, 256], P('ctx')
- grad_dt_raw: float32 [128, 2048], P('head', 'ctx')
The draws below stay inside these ranges and needn't reach their ends.
Inputs may be any that keep to these rules, and one draw needn't show every extreme that they name: Block b holds a document start at row 256 * b + doc_starts[b] when doc_starts[b] < 256, and none when doc_starts[b] = 256; doc_starts[0] = 0.
All inputs are finite; a program needn't handle non-finite values.
Results may differ from the reference program's by a relative error of at most 0.013.
Values may be sent and summed in bfloat16 or wider, within the bound.
A program may use at most 128 MiB of HBM per device.

```python
import math
import jax
import jax.numpy as jnp
from jax import lax

ATTENTION_COUNT = 128
STATE = 128
KERNEL = 4
BLOCK = 256
TOK_DEV = 256
TOKEN_LENGTH = 2048
NBLOCKS = 8
CHANNELS = 8192


def draw_a_log(key, part):
    lowest = math.log(1.0 / TOK_DEV)
    highest = math.log(2.0)
    return jax.random.uniform(key, (ATTENTION_COUNT,), jnp.float32, lowest, highest)


def draw_dt_raw(key, part):
    key_base = jax.random.fold_in(key, 11)
    random_seed_batch = jax.random.fold_in(key, 12)
    key_level = jax.random.fold_in(key, 13)
    starting_index = jnp.clip(-4.0 + 0.7 * jax.random.normal(key_base, (ATTENTION_COUNT, TOKEN_LENGTH), jnp.float32), -6.5, -1.5)
    parallel_batch = jax.random.uniform(random_seed_batch, (ATTENTION_COUNT, TOKEN_LENGTH), jnp.float32) < 1.0 / 128.0
    layer_index = jax.random.uniform(key_level, (ATTENTION_COUNT, TOKEN_LENGTH), jnp.float32, -1.0, 0.0)
    return jnp.where(parallel_batch, layer_index, starting_index)


def draw_doc_starts(key, part):
    key_pick = jax.random.fold_in(key, 21)
    key_for_spot = jax.random.fold_in(key, 22)
    picked = jax.random.randint(key_pick, (NBLOCKS,), 0, 8)
    spot = jax.random.randint(key_for_spot, (NBLOCKS,), 0, BLOCK)
    values = jnp.where(picked == 0, spot, BLOCK)
    values = jnp.where(jnp.arange(NBLOCKS) == 0, 0, values)
    return values.astype(jnp.int32)


def block_levels(key, dims, split, low, top_value):
    gain, own = 1.0, jax.random.fold_in(key, 6)
    for axis_at, blocks in split:
        draws = jnp.exp(jax.random.uniform(jax.random.fold_in(own, axis_at), (blocks,), jnp.float32, low / len(split), top_value / len(split)))
        gain = gain * jnp.repeat(draws, dims[axis_at] // blocks).reshape([-1 if axis == axis_at else 1 for axis in range(len(dims))])
    return gain


def normal_values(stream_key, shape, spread, bound, split=(), held_as=jnp.bfloat16):
    values = spread * jax.random.normal(stream_key, shape, jnp.float32)
    if split:
        values = values * block_levels(stream_key, shape, split, -0.22, 0.18)
    return jnp.clip(values, -bound, bound).astype(held_as)


def setup_inputs(seed: int = 0) -> dict:
    key_list = jax.random.split(jax.random.key(seed), 10)
    x_raw = normal_values(key_list[0], (TOKEN_LENGTH, CHANNELS), 1.0, 6.0, ((0, 8), (1, 4)))
    bc_raw = normal_values(key_list[1], (TOKEN_LENGTH, 2 * STATE), 1.0, 6.0, ((0, 8),))
    conv_x_w = normal_values(key_list[2], (KERNEL, CHANNELS), KERNEL ** -0.5, 3.0, ((1, 4),))
    conv_bc_w = normal_values(key_list[3], (KERNEL, 2 * STATE), KERNEL ** -0.5, 3.0)
    dt_raw = draw_dt_raw(jax.random.fold_in(key_list[9], 71), 0)
    a_log = draw_a_log(jax.random.fold_in(key_list[9], 71), 0)
    d_skip = jnp.clip(0.5 + 1.0 * jax.random.uniform(key_list[6], (ATTENTION_COUNT,), jnp.float32) ** block_levels(key_list[6], (ATTENTION_COUNT,), ((0, 4),), -0.2, 0.2), 0.5, 1.5)
    doc_starts = draw_doc_starts(jax.random.fold_in(key_list[9], 71), 0)
    grad_y = normal_values(key_list[8], (TOKEN_LENGTH, CHANNELS), 1.0, 6.0, ((0, 8), (1, 4)))
    return dict(x_raw=x_raw, bc_raw=bc_raw, conv_x_w=conv_x_w, conv_bc_w=conv_bc_w, dt_raw=dt_raw, a_log=a_log, d_skip=d_skip, doc_starts=doc_starts, grad_y=grad_y)


def contract(pattern, first_op, second_op):
    return jnp.einsum(pattern, first_op.astype(jnp.float32), second_op.astype(jnp.float32))

def contract_exact(pattern, first_op, second_op):
    return jnp.einsum(pattern, first_op.astype(jnp.float32), second_op.astype(jnp.float32), precision=lax.Precision.HIGHEST)

def silu_grad(values):
    sigmoid_v = jax.nn.sigmoid(values)
    return sigmoid_v * (1.0 + values * (1.0 - sigmoid_v))

def causal_conv(tok_rows, before, weight):
    row_count = tok_rows.shape[0]
    tap_count = weight.shape[0]
    padded = jnp.concatenate([before, tok_rows], axis=0).astype(jnp.float32)
    weight_f = weight.astype(jnp.float32)
    running = jnp.zeros(tok_rows.shape, jnp.float32)
    for offset in range(tap_count):
        running = running + weight_f[offset] * padded[offset:offset + row_count]
    return running

def conv_back(gradient, following, weight):
    row_count = gradient.shape[0]
    tap_count = weight.shape[0]
    padded = jnp.concatenate([gradient, following], axis=0)
    weight_f = weight.astype(jnp.float32)
    running = jnp.zeros(gradient.shape, jnp.float32)
    for offset in range(tap_count):
        running = running + weight_f[tap_count - 1 - offset] * padded[offset:offset + row_count]
    return running

def block_prep(x_block, bc_block, step_block, decay_rate, reset_at):
    block_len = step_block.shape[1]
    nstate = bc_block.shape[1] // 2
    position = jnp.arange(block_len, dtype=jnp.int32)
    segment = position >= reset_at
    cumulated = jnp.cumsum(-decay_rate[:, None] * step_block, axis=1)
    causal = (segment[:, None] == segment[None, :]) & (position[:, None] >= position[None, :])
    kernel = jnp.exp(jnp.where(causal[None], cumulated[:, :, None] - cumulated[:, None, :], -jnp.inf))
    entering = jnp.where(segment[None, :], 0.0, jnp.exp(cumulated))
    final_cum = cumulated[:, block_len - 1:]
    leaving = jnp.where(segment[None, :] == segment[block_len - 1], jnp.exp(final_cum - cumulated), 0.0)
    carry_out = jnp.where(reset_at >= block_len, jnp.exp(cumulated[:, block_len - 1]), 0.0)
    b_matrix = bc_block[:, :nstate]
    c_matrix = bc_block[:, nstate:]
    gram_mat = contract('tn,sn->ts', c_matrix, b_matrix)
    mixing = (gram_mat[None] * kernel).astype(jnp.bfloat16)
    x_float = x_block.astype(jnp.float32)
    scaled_x = (x_float * jnp.transpose(step_block)[:, :, None]).astype(jnp.bfloat16)
    leaving_x = (x_float * jnp.transpose(leaving * step_block)[:, :, None]).astype(jnp.bfloat16)
    return dict(kernel=kernel, entering=entering, leaving=leaving, carry_out=carry_out, b_matrix=b_matrix, c_matrix=c_matrix, gram_mat=gram_mat, mixing=mixing, scaled_x=scaled_x, leaving_x=leaving_x)

def block_state(prepared):
    return contract('shp,sn->hpn', prepared['leaving_x'], prepared['b_matrix'])

def block_out(prepared, x_block, d_skip, state_in):
    state_q = state_in.astype(jnp.bfloat16)
    intra = contract('hts,shp->thp', prepared['mixing'], prepared['scaled_x'])
    y_state = contract('tn,hpn->thp', prepared['c_matrix'], state_q)
    result = intra + jnp.transpose(prepared['entering'])[:, :, None] * y_state + d_skip[None, :, None] * x_block.astype(jnp.float32)
    return (result.astype(jnp.bfloat16), y_state)

def block_bsum(prepared, output_grad_block):
    enter_dy = (output_grad_block.astype(jnp.float32) * jnp.transpose(prepared['entering'])[:, :, None]).astype(jnp.bfloat16)
    return (enter_dy, contract('thp,tn->hpn', enter_dy, prepared['c_matrix']))

def block_back(prepared, x_block, output_grad_block, enter_dy, y_state, state_in, dstate, decay_rate, d_skip, step_block):
    block_len = step_block.shape[1]
    kernel = prepared['kernel']
    dstate_q = dstate.astype(jnp.bfloat16)
    state_q = state_in.astype(jnp.bfloat16)
    response = contract('thp,shp->hts', output_grad_block, prepared['scaled_x'])
    weighed = response * kernel
    z_term = weighed * prepared['gram_mat'][None]
    d_gram = lax.optimization_barrier(jnp.sum(weighed, axis=0))
    grad_c = contract_exact('ts,sn->tn', d_gram, prepared['b_matrix']) + contract('thp,hpn->tn', enter_dy, state_q)
    grad_b = contract_exact('ts,tn->sn', d_gram, prepared['c_matrix']) + contract('shp,hpn->sn', prepared['leaving_x'], dstate_q)
    d_scaled = contract('hts,thp->shp', prepared['mixing'], output_grad_block)
    d_leaving = contract('sn,hpn->shp', prepared['b_matrix'], dstate_q)
    x_float = x_block.astype(jnp.float32)
    step_t = jnp.transpose(step_block)
    leave_t = jnp.transpose(prepared['leaving'])
    grad_xc = step_t[:, :, None] * d_scaled + (leave_t * step_t)[:, :, None] * d_leaving + d_skip[None, :, None] * output_grad_block.astype(jnp.float32)
    along_dt = jnp.transpose(lax.optimization_barrier(jnp.sum(x_float * d_scaled, axis=2)))
    along_leave = jnp.transpose(lax.optimization_barrier(jnp.sum(x_float * d_leaving, axis=2)))
    leave_term = prepared['leaving'] * step_block * along_leave
    enter_term = prepared['entering'] * jnp.transpose(lax.optimization_barrier(jnp.sum(output_grad_block.astype(jnp.float32) * y_state, axis=2)))
    final_term = lax.optimization_barrier(jnp.sum(leave_term, axis=1)) + prepared['carry_out'] * lax.optimization_barrier(jnp.sum(dstate * state_in, axis=(1, 2)))
    is_final = jnp.arange(block_len, dtype=jnp.int32) == block_len - 1
    d_cum = lax.optimization_barrier(jnp.sum(z_term, axis=2)) - lax.optimization_barrier(jnp.sum(z_term, axis=1)) + enter_term - leave_term
    d_cum = d_cum + jnp.where(is_final[None, :], final_term[:, None], 0.0)
    d_log = lax.cumsum(d_cum, axis=1, reverse=True)
    grad_step = along_dt + prepared['leaving'] * along_leave - decay_rate[:, None] * d_log
    return (grad_b, grad_c, grad_xc, grad_step)

def reference(x_raw, bc_raw, conv_x_w, conv_bc_w, dt_raw, a_log, d_skip, doc_starts, grad_y):
    seq_len, channels = x_raw.shape
    head_count = a_log.shape[0]
    head_dim = channels // head_count
    nstate = bc_raw.shape[1] // 2
    rim_rows = conv_x_w.shape[0] - 1
    x_pre = causal_conv(x_raw, jnp.zeros((rim_rows, channels), x_raw.dtype), conv_x_w)
    bc_pre = causal_conv(bc_raw, jnp.zeros((rim_rows, 2 * nstate), bc_raw.dtype), conv_bc_w)
    x_conv = jax.nn.silu(x_pre).astype(jnp.bfloat16)
    bc_conv = jax.nn.silu(bc_pre).astype(jnp.bfloat16)
    step_size = jax.nn.softplus(dt_raw)
    decay_rate = jnp.exp(a_log)
    nblock = seq_len // BLOCK
    x_blocks = x_conv.reshape(nblock, BLOCK, head_count, head_dim)
    bc_blocks = bc_conv.reshape(nblock, BLOCK, 2 * nstate)
    step_blocks = jnp.transpose(step_size.reshape(head_count, nblock, BLOCK), (1, 0, 2))
    dy_blocks = grad_y.reshape(nblock, BLOCK, head_count, head_dim)
    zero_state = jnp.zeros((head_count, head_dim, nstate), jnp.float32)

    def forward_step(state_in, inputs):
        x_block, bc_block, step_block, reset_at = inputs
        prepared = block_prep(x_block, bc_block, step_block, decay_rate, reset_at)
        y_block, unused_state = block_out(prepared, x_block, d_skip, state_in)
        state_out = prepared['carry_out'][:, None, None] * state_in + block_state(prepared)
        return (state_out, (y_block, state_in))
    unused_final, (y_blocks, state_blocks) = lax.scan(forward_step, zero_state, (x_blocks, bc_blocks, step_blocks, doc_starts))

    def backward_step(dstate, inputs):
        x_block, bc_block, step_block, reset_at, output_grad_block, state_in = inputs
        prepared = block_prep(x_block, bc_block, step_block, decay_rate, reset_at)
        enter_dy, back_part = block_bsum(prepared, output_grad_block)
        unused_y, y_state = block_out(prepared, x_block, d_skip, state_in)
        grads = block_back(prepared, x_block, output_grad_block, enter_dy, y_state, state_in, dstate, decay_rate, d_skip, step_block)
        dstate_in = prepared['carry_out'][:, None, None] * dstate + back_part
        return (dstate_in, grads)
    unused_first, (grad_bs, grad_cs, filtered_input_cotangents, grad_steps) = lax.scan(backward_step, zero_state, (x_blocks, bc_blocks, step_blocks, doc_starts, dy_blocks, state_blocks), reverse=True)
    grad_bc = jnp.concatenate([grad_bs.reshape(seq_len, nstate), grad_cs.reshape(seq_len, nstate)], axis=1)
    grad_bc_pre = grad_bc * silu_grad(bc_pre)
    grad_x_pre = filtered_input_cotangents.reshape(seq_len, channels) * silu_grad(x_pre)
    grad_x_raw = conv_back(grad_x_pre, jnp.zeros((rim_rows, channels), jnp.float32), conv_x_w).astype(jnp.bfloat16)
    grad_bc_raw = conv_back(grad_bc_pre, jnp.zeros((rim_rows, 2 * nstate), jnp.float32), conv_bc_w).astype(jnp.bfloat16)
    grad_step = jnp.transpose(grad_steps, (1, 0, 2)).reshape(head_count, seq_len)
    grad_dt_raw = grad_step * jax.nn.sigmoid(dt_raw)
    y_out = y_blocks.reshape(seq_len, channels)
    return (y_out, grad_x_raw, grad_bc_raw, grad_dt_raw)
```

```python
import functools

import jax
import jax.numpy as jnp
from jax import lax
from jax.experimental import pallas as pl
from jax.experimental.pallas import tpu as pltpu
from jax.sharding import PartitionSpec as P

F32 = jnp.float32
BF16 = jnp.bfloat16
LANES = 128
RIM = 16


def dot_nn(a, b):
    return lax.dot_general(a, b, (((1,), (0,)), ((), ())), preferred_element_type=F32)


def dot_nt(a, b):
    return lax.dot_general(a, b, (((1,), (1,)), ((), ())), preferred_element_type=F32)


def dot_tn(a, b):
    return lax.dot_general(a, b, (((0,), (0,)), ((), ())), preferred_element_type=F32)


def exact_nn(a, b):
    return lax.dot_general(
        a, b, (((1,), (0,)), ((), ())), precision=lax.Precision.HIGHEST, preferred_element_type=F32
    )


def halves(value):
    top = value.astype(BF16)
    return top, (value - top.astype(F32)).astype(BF16)


def sigmoid(v):
    return 1.0 / (1.0 + jnp.exp(-v))


def kernel(
    n_ctx, n_head, pairs,
    x_ref, bc_ref, wx_ref, wbc_ref, dt_ref, alog_ref, dskip_ref, doc_ref, dy_ref,
    y_ref, gx_ref, gbc_ref, gdt_ref,
    halo_x, halo_bc, xp, bcp, stat, s_ref, g_ref, cexp, fin, fout, bin_, bout,
    xc, sx, lx, edy, sgrad, intra, dsc, step_l, leave_l, enter_l, gp, gbp, sgrad_bc,
    b_mat, c_mat, gram, bias, dgram, gb_acc, gc_acc, rr, cs, parts, nxt_x, nxt_bc,
    hx_send, hx_recv, hb_send, hb_recv, f_send, f_recv, b_send, b_recv,
    p_send, p_recv, nx_send, nx_recv, nb_send, nb_recv,
):
    rows = x_ref.shape[0]
    heads = dt_ref.shape[0]
    nstate = bc_ref.shape[1] // 2
    taps = wx_ref.shape[0]
    ctx = lax.axis_index("ctx")
    head = lax.axis_index("head")
    has_prev = ctx > 0
    has_next = ctx < n_ctx - 1
    half = LANES // 2

    barrier = pltpu.get_barrier_semaphore()

    @pl.when(has_prev)
    def _():
        pl.semaphore_signal(barrier, inc=1, device_id=(ctx - 1, head), device_id_type=pl.DeviceIdType.MESH)

    @pl.when(has_next)
    def _():
        pl.semaphore_signal(barrier, inc=1, device_id=(ctx + 1, head), device_id_type=pl.DeviceIdType.MESH)

    for off in range(1, n_head):
        pl.semaphore_signal(
            barrier, inc=1, device_id=(ctx, lax.rem(head + off, n_head)), device_id_type=pl.DeviceIdType.MESH
        )

    inside = has_prev & has_next

    @pl.when(inside)
    def _():
        pl.semaphore_wait(barrier, n_head + 1)

    @pl.when(jnp.logical_not(inside))
    def _():
        pl.semaphore_wait(barrier, n_head)

    def remote(src, dst, send, recv, to):
        return pltpu.make_async_remote_copy(
            src_ref=src, dst_ref=dst, send_sem=send, recv_sem=recv, device_id=to,
            device_id_type=pl.DeviceIdType.MESH,
        )

    after = (ctx + 1, head)
    before = (ctx - 1, head)
    x_halo = remote(x_ref.at[pl.ds(rows - RIM, RIM)], halo_x, hx_send, hx_recv, after)
    bc_halo = remote(bc_ref.at[pl.ds(rows - RIM, RIM)], halo_bc, hb_send, hb_recv, after)

    @pl.when(has_next)
    def _():
        bc_halo.start()
        x_halo.start()

    doc = doc_ref[0]
    dt = dt_ref[...]
    step = jnp.maximum(dt, 0.0) + jnp.log(1.0 + jnp.exp(-jnp.abs(dt)))
    decay = jnp.exp(alog_ref[...])
    r_id = lax.broadcasted_iota(jnp.int32, (rows, rows), 0)
    c_id = lax.broadcasted_iota(jnp.int32, (rows, rows), 1)
    same = (r_id >= doc) == (c_id >= doc)
    bias[...] = jnp.where(same & (r_id >= c_id), 0.0, -1e30)
    cum = exact_nn(-decay * step, jnp.where(r_id <= c_id, 1.0, 0.0))
    pos = lax.broadcasted_iota(jnp.int32, (heads, rows), 1)
    part = pos >= doc
    last_part = (rows - 1) >= doc
    enter = jnp.where(part, 0.0, jnp.exp(cum))
    final = cum[:, rows - 1 :]
    leave = jnp.where(part == last_part, jnp.exp(final - cum), 0.0)
    for k in range(pairs):
        pick = slice(2 * k, 2 * k + 2)
        stat[k, 0:2, :] = cum[pick]
        stat[k, 2:4, :] = step[pick]
        stat[k, 4:6, :] = leave[pick]
        stat[k, 6:8, :] = enter[pick]
    dgram[...] = jnp.zeros_like(dgram)
    gb_acc[...] = jnp.zeros_like(gb_acc)
    gc_acc[...] = jnp.zeros_like(gc_acc)

    @pl.when(has_next)
    def _():
        bc_halo.wait_send()
        x_halo.wait_send()

    @pl.when(has_prev)
    def _():
        bc_halo.wait_recv()
        x_halo.wait_recv()

    @pl.when(jnp.logical_not(has_prev))
    def _():
        halo_x[...] = jnp.zeros_like(halo_x)
        halo_bc[...] = jnp.zeros_like(halo_bc)
        fin[...] = jnp.zeros_like(fin)

    @pl.when(jnp.logical_not(has_next))
    def _():
        nxt_x[...] = jnp.zeros_like(nxt_x)
        nxt_bc[...] = jnp.zeros_like(nxt_bc)
        bin_[...] = jnp.zeros_like(bin_)

    def conv(pad_ref, weight):
        total = weight[0:1] * pad_ref[9 - taps : 9 - taps + rows, :]
        for tap in range(1, taps):
            at = 9 - taps + tap
            total = total + weight[tap : tap + 1] * pad_ref[at : at + rows, :]
        return total

    bcp[0:8, :] = halo_bc[RIM - 8 :, :].astype(F32)
    bcp[8:, :] = bc_ref[...].astype(F32)
    bc_pre = conv(bcp, wbc_ref[...].astype(F32))
    sig = sigmoid(bc_pre)
    bc_conv = (bc_pre * sig).astype(BF16)
    sgrad_bc[...] = sig * (1.0 + bc_pre * (1.0 - sig))
    b_mat[...] = bc_conv[:, :nstate]
    c_mat[...] = bc_conv[:, nstate:]
    gram[...] = dot_nt(bc_conv[:, nstate:], bc_conv[:, :nstate])

    lane = lax.broadcasted_iota(jnp.int32, (rows, LANES), 1)
    low = lane < half
    carry_on = doc >= rows

    def spread(columns, at):
        return jnp.where(low, columns[:, at : at + 1], columns[:, at + 1 : at + 2])

    def prepare(k):
        cols = pl.ds(pl.multiple_of(k * LANES, LANES), LANES)
        turned = jnp.transpose(stat[k])
        step_k = spread(turned, 2)
        leave_k = spread(turned, 4)
        enter_k = spread(turned, 6)
        step_l[:, cols] = step_k
        leave_l[:, cols] = leave_k
        enter_l[:, cols] = enter_k
        xp[0:8, :] = halo_x[RIM - 8 :, cols].astype(F32)
        xp[8:, :] = x_ref[:, cols].astype(F32)
        pre = conv(xp, wx_ref[:, cols].astype(F32))
        sig_k = sigmoid(pre)
        sgrad[:, cols] = sig_k * (1.0 + pre * (1.0 - sig_k))
        xb = (pre * sig_k).astype(BF16)
        xc[:, cols] = xb
        xf = xb.astype(F32)
        sx[:, cols] = (xf * step_k).astype(BF16)
        lx_k = (xf * (leave_k * step_k)).astype(BF16)
        lx[:, cols] = lx_k
        edy_k = (dy_ref[:, cols].astype(F32) * enter_k).astype(BF16)
        edy[:, cols] = edy_k
        s_ref[k] = dot_tn(lx_k, b_mat[...])
        g_ref[k] = dot_tn(edy_k, c_mat[...])
        ends = jnp.where(carry_on, jnp.exp(turned[rows - 1 : rows, 0:2]), 0.0)
        cexp[k, 0:half, :] = jnp.broadcast_to(ends[:, 0:1], (half, LANES))
        cexp[k, half:, :] = jnp.broadcast_to(ends[:, 1:2], (half, LANES))

    def chain(i):
        kf = i - ctx

        @pl.when((kf >= 0) & (kf < pairs))
        def _():
            @pl.when(has_prev)
            def _():
                remote(fout.at[kf], fin.at[kf], f_send.at[kf], f_recv.at[kf], after).wait_recv()

            @pl.when(has_next)
            def _():
                fout[kf] = (fin[kf].astype(F32) * cexp[kf] + s_ref[kf]).astype(BF16)
                remote(fout.at[kf], fin.at[kf], f_send.at[kf], f_recv.at[kf], after).start()

        kb = i - (n_ctx - 1 - ctx)

        @pl.when((kb >= 0) & (kb < pairs))
        def _():
            @pl.when(has_next)
            def _():
                remote(bout.at[kb], bin_.at[kb], b_send.at[kb], b_recv.at[kb], before).wait_recv()

            @pl.when(has_prev)
            def _():
                bout[kb] = (bin_[kb].astype(F32) * cexp[kb] + g_ref[kb]).astype(BF16)
                remote(bout.at[kb], bin_.at[kb], b_send.at[kb], b_recv.at[kb], before).start()

    def heavy(k):
        cols = pl.ds(pl.multiple_of(k * LANES, LANES), LANES)
        turned = jnp.transpose(stat[k])
        sx_k = sx[:, cols]
        dy_k = dy_ref[:, cols]
        zero = jnp.zeros_like(sx_k)
        outs, backs, weighs = [], [], []
        for j in range(2):
            mine = low if j == 0 else jnp.logical_not(low)
            ker = jnp.exp((turned[:, j : j + 1] - stat[k, j : j + 1, :]) + bias[...])
            mixing = (gram[...] * ker).astype(BF16)
            response = dot_nt(dy_k, jnp.where(mine, sx_k, zero))
            weighs.append(response * ker)
            outs.append(dot_nn(mixing, sx_k))
            backs.append(dot_tn(mixing, dy_k))
        dgram[...] += weighs[0] + weighs[1]
        intra[:, cols] = jnp.where(low, outs[0], outs[1])
        dsc[:, cols] = jnp.where(low, backs[0], backs[1])

    @pl.loop(0, pairs + n_ctx - 1)
    def _(i):
        @pl.when(i < pairs)
        def _():
            prepare(i)

        chain(i)

        @pl.when(i < pairs)
        def _():
            heavy(i)

    e_row = lax.broadcasted_iota(jnp.int32, (8, LANES), 0)
    e_col = lax.broadcasted_iota(jnp.int32, (8, LANES), 1) // half

    def finish(k):
        cols = pl.ds(pl.multiple_of(k * LANES, LANES), LANES)
        st = fin[k]
        ds = bin_[k]
        skip = dskip_ref[:, cols]
        step_k = step_l[:, cols]
        leave_k = leave_l[:, cols]
        xf = xc[:, cols].astype(F32)
        dyf = dy_ref[:, cols].astype(F32)
        dsc_k = dsc[:, cols]
        y_all = intra[:, cols] + enter_l[:, cols] * dot_nt(c_mat[...], st)
        y_ref[:, cols] = (y_all + skip * xf).astype(BF16)
        dlv = leave_k * dot_nt(b_mat[...], ds)
        both = dsc_k + dlv
        gp[0:rows, cols] = (step_k * both + skip * dyf) * sgrad[:, cols]
        gc_acc[...] += dot_nn(edy[:, cols], st)
        gb_acc[...] += dot_nn(lx[:, cols], ds)
        lterm = step_k * xf * dlv
        u1 = dyf * y_all - sx[:, cols].astype(F32) * dsc_k - lterm
        total = jnp.zeros((8, rows), F32)
        for at, value in ((0, u1), (2, xf * both), (4, lterm)):
            ones = jnp.where(e_row == e_col + at, 1.0, 0.0).astype(BF16)
            top, rest = halves(value)
            total = total + (dot_nt(ones, top) + dot_nt(ones, rest))
        rr[k] = total
        both_states = st.astype(F32) * ds.astype(F32) * cexp[k]
        cs[k, 0:1, :] = jnp.sum(both_states[0:half], axis=0, keepdims=True)
        cs[k, 1:2, :] = jnp.sum(both_states[half:], axis=0, keepdims=True)

    pl.loop(0, pairs)(finish)

    x_rim = remote(gp.at[pl.ds(0, 8)], nxt_x, nx_send, nx_recv, before)

    @pl.when(has_prev)
    def _():
        x_rim.start()

    top, rest = halves(dgram[...])
    grad_c = gc_acc[...] + dot_nn(top, b_mat[...]) + dot_nn(rest, b_mat[...])
    grad_b = gb_acc[...] + dot_tn(top, c_mat[...]) + dot_tn(rest, c_mat[...])
    parts[head, :, 0:nstate] = grad_b.astype(BF16)
    parts[head, :, nstate:] = grad_c.astype(BF16)
    sends = []
    for off in range(1, n_head):
        to = (ctx, lax.rem(head + off, n_head))
        copy = remote(parts.at[head], parts.at[head], p_send.at[off - 1], p_recv.at[off - 1], to)
        copy.start()
        sends.append(copy)

    tri = jnp.where(r_id >= c_id, 1.0, 0.0)
    dt_sig = sigmoid(dt)
    pos2 = lax.broadcasted_iota(jnp.int32, (2, rows), 1) == rows - 1
    cums, direct = [], []
    for k in range(pairs):
        extra = jnp.sum(rr[k, 4:6, :], axis=1, keepdims=True) + jnp.sum(cs[k, 0:2, :], axis=1, keepdims=True)
        cums.append(rr[k, 0:2, :] + jnp.where(pos2, extra, 0.0))
        direct.append(rr[k, 2:4, :])
    d_log = exact_nn(jnp.concatenate(cums, axis=0), tri)
    gdt_ref[...] = (jnp.concatenate(direct, axis=0) - decay * d_log) * dt_sig

    @pl.when(has_next)
    def _():
        x_rim.wait_recv()

    gp[rows:, :] = nxt_x[...]

    @pl.loop(0, pairs)
    def _(k):
        cols = pl.ds(pl.multiple_of(k * LANES, LANES), LANES)
        weight = wx_ref[:, cols].astype(F32)
        total = weight[taps - 1 : taps] * gp[0:rows, cols]
        for off in range(1, taps):
            total = total + weight[taps - 1 - off : taps - off] * gp[off : off + rows, cols]
        gx_ref[:, cols] = total.astype(BF16)

    for off in range(1, n_head):
        source = lax.rem(head + n_head - off, n_head)
        remote(
            parts.at[source], parts.at[source], p_send.at[off - 1], p_recv.at[off - 1],
            (ctx, lax.rem(head + off, n_head)),
        ).wait_recv()
    total = parts[0].astype(F32)
    for other in range(1, n_head):
        total = total + parts[other].astype(F32)
    gbp[0:rows, :] = total * sgrad_bc[...]
    bc_rim = remote(gbp.at[pl.ds(0, 8)], nxt_bc, nb_send, nb_recv, before)

    @pl.when(has_prev)
    def _():
        bc_rim.start()

    for copy in sends:
        copy.wait_send()

    @pl.loop(0, pairs)
    def _(k):
        @pl.when(has_next)
        def _():
            remote(fout.at[k], fin.at[k], f_send.at[k], f_recv.at[k], after).wait_send()

        @pl.when(has_prev)
        def _():
            remote(bout.at[k], bin_.at[k], b_send.at[k], b_recv.at[k], before).wait_send()

    @pl.when(has_next)
    def _():
        bc_rim.wait_recv()

    gbp[rows:, :] = nxt_bc[...]
    weight = wbc_ref[...].astype(F32)
    total = weight[taps - 1 : taps] * gbp[0:rows, :]
    for off in range(1, taps):
        total = total + weight[taps - 1 - off : taps - off] * gbp[off : off + rows, :]
    gbc_ref[...] = total.astype(BF16)

    @pl.when(has_prev)
    def _():
        x_rim.wait_send()
        bc_rim.wait_send()


def body(n_ctx, n_head, x_raw, bc_raw, conv_x_w, conv_bc_w, dt_raw, a_log, d_skip, doc_starts, grad_y):
    rows, channels = x_raw.shape
    heads = a_log.shape[0]
    nstate = bc_raw.shape[1] // 2
    pairs = channels // LANES
    vmem = pl.BlockSpec(memory_space=pltpu.VMEM)
    smem = pl.BlockSpec(memory_space=pltpu.SMEM)
    wide = pltpu.VMEM((rows, channels), F32)
    wide_h = pltpu.VMEM((rows, channels), BF16)
    state = pltpu.VMEM((pairs, LANES, nstate), F32)
    state_h = pltpu.VMEM((pairs, LANES, nstate), BF16)
    dma = pltpu.SemaphoreType.DMA
    scratch = [
        pltpu.VMEM((RIM, channels), BF16),
        pltpu.VMEM((RIM, 2 * nstate), BF16),
        pltpu.VMEM((rows + 8, LANES), F32),
        pltpu.VMEM((rows + 8, 2 * nstate), F32),
        pltpu.VMEM((pairs, 8, rows), F32),
        state, state, state,
        state_h, state_h, state_h, state_h,
        wide_h, wide_h, wide_h, wide_h,
        wide, wide, wide, wide, wide, wide,
        pltpu.VMEM((rows + 8, channels), F32),
        pltpu.VMEM((rows + 8, 2 * nstate), F32),
        pltpu.VMEM((rows, 2 * nstate), F32),
        pltpu.VMEM((rows, nstate), BF16),
        pltpu.VMEM((rows, nstate), BF16),
        pltpu.VMEM((rows, rows), F32),
        pltpu.VMEM((rows, rows), F32),
        pltpu.VMEM((rows, rows), F32),
        pltpu.VMEM((rows, nstate), F32),
        pltpu.VMEM((rows, nstate), F32),
        pltpu.VMEM((pairs, 8, rows), F32),
        pltpu.VMEM((pairs, 8, LANES), F32),
        pltpu.VMEM((n_head, rows, 2 * nstate), BF16),
        pltpu.VMEM((8, channels), F32),
        pltpu.VMEM((8, 2 * nstate), F32),
        dma, dma, dma, dma,
        dma((pairs,)), dma((pairs,)), dma((pairs,)), dma((pairs,)),
        dma((n_head - 1,)), dma((n_head - 1,)),
        dma, dma, dma, dma,
    ]
    return pl.pallas_call(
        functools.partial(kernel, n_ctx, n_head, pairs),
        out_shape=(
            jax.ShapeDtypeStruct((rows, channels), BF16),
            jax.ShapeDtypeStruct((rows, channels), BF16),
            jax.ShapeDtypeStruct((rows, 2 * nstate), BF16),
            jax.ShapeDtypeStruct((heads, rows), F32),
        ),
        in_specs=[vmem] * 7 + [smem, vmem],
        out_specs=(vmem, vmem, vmem, vmem),
        scratch_shapes=scratch,
        compiler_params=pltpu.CompilerParams(
            collective_id=0, has_side_effects=True, vmem_limit_bytes=56 * 1024 * 1024
        ),
        cost_estimate=pl.CostEstimate(flops=3 * 10**9, bytes_accessed=6 * 2**20, transcendentals=3 * 10**6),
    )(
        x_raw, bc_raw, conv_x_w, conv_bc_w, dt_raw, a_log[:, None],
        jnp.repeat(d_skip, channels // heads)[None, :], doc_starts, grad_y,
    )


def solution(mesh):
    in_specs = (
        P("ctx", "head"),
        P("ctx", None),
        P(None, "head"),
        P(),
        P("head", "ctx"),
        P("head"),
        P("head"),
        P("ctx"),
        P("ctx", "head"),
    )
    out_specs = (P("ctx", "head"), P("ctx", "head"), P("ctx", None), P("head", "ctx"))
    inner = functools.partial(body, mesh.shape["ctx"], mesh.shape["head"])
    return jax.shard_map(inner, mesh=mesh, in_specs=in_specs, out_specs=out_specs, check_vma=False)
```

```python
import functools

import jax
import jax.numpy as jnp
from jax import lax
from jax.experimental import pallas as pl
from jax.experimental.pallas import tpu as pltpu
from jax.sharding import PartitionSpec as P

F32 = jnp.float32
BF16 = jnp.bfloat16
LANES = 128
RIM = 16
LAG = 2


def dot_nn(a, b):
    return lax.dot_general(a, b, (((1,), (0,)), ((), ())), preferred_element_type=F32)


def dot_nt(a, b):
    return lax.dot_general(a, b, (((1,), (1,)), ((), ())), preferred_element_type=F32)


def dot_tn(a, b):
    return lax.dot_general(a, b, (((0,), (0,)), ((), ())), preferred_element_type=F32)


def exact_nn(a, b):
    return lax.dot_general(
        a, b, (((1,), (0,)), ((), ())), precision=lax.Precision.HIGHEST, preferred_element_type=F32
    )


def halves(value):
    top = value.astype(BF16)
    return top, (value - top.astype(F32)).astype(BF16)


def sigmoid(v):
    return 1.0 / (1.0 + jnp.exp(-v))


def kernel(
    n_ctx, n_head, pairs,
    x_ref, bc_ref, wx_ref, wbc_ref, dt_ref, alog_ref, dskip_ref, doc_ref, dy_ref,
    y_ref, gx_ref, gbc_ref, gdt_ref,
    halo_x, halo_bc, xp, bcp, stat, s_ref, g_ref, carry_own, carry_oth,
    s_out, s_in, g_out, g_in, fin, fout, bin_, bout, z_in, z_out, r_in, r_out,
    xc, sx, lx, edy, sgrad, intra, dsc, step_l, leave_l, enter_l, gp, gbp, sgrad_bc,
    b_mat, c_mat, gram, bias, dgram, gb_acc, gc_acc, rr, cs, parts, nxt_x, nxt_bc,
    hx_send, hx_recv, hb_send, hb_recv, f_send, f_recv, b_send, b_recv, c_send, c_recv,
    s_send, s_recv, g_send, g_recv, z_send, z_recv, r_send, r_recv,
    p_send, p_recv, nx_send, nx_recv, nb_send, nb_recv,
):
    rows = x_ref.shape[0]
    heads = dt_ref.shape[0]
    nstate = bc_ref.shape[1] // 2
    taps = wx_ref.shape[0]
    ctx = lax.axis_index("ctx")
    head = lax.axis_index("head")
    has_prev = ctx > 0
    has_next = ctx < n_ctx - 1
    half = LANES // 2

    barrier = pltpu.get_barrier_semaphore()

    for dist in (1, 2):
        for sign in (-1, 1):

            @pl.when((ctx + sign * dist >= 0) & (ctx + sign * dist < n_ctx))
            def _(dist=dist, sign=sign):
                pl.semaphore_signal(
                    barrier, inc=1, device_id=(ctx + sign * dist, head), device_id_type=pl.DeviceIdType.MESH
                )

    for off in range(1, n_head):
        pl.semaphore_signal(
            barrier, inc=1, device_id=(ctx, lax.rem(head + off, n_head)), device_id_type=pl.DeviceIdType.MESH
        )

    for lows in range(3):
        for highs in range(3):
            is_low = ctx == lows if lows < 2 else ctx >= 2
            left = n_ctx - 1 - ctx
            is_high = left == highs if highs < 2 else left >= 2

            @pl.when(is_low & is_high)
            def _(count=lows + highs + n_head - 1):
                pl.semaphore_wait(barrier, count)

    def remote(src, dst, send, recv, to):
        return pltpu.make_async_remote_copy(
            src_ref=src, dst_ref=dst, send_sem=send, recv_sem=recv, device_id=to,
            device_id_type=pl.DeviceIdType.MESH,
        )

    after = (ctx + 1, head)
    before = (ctx - 1, head)
    side = lax.rem(ctx, 2)
    first = side == 0
    duo = ctx // 2
    duos = n_ctx // 2
    partner = (ctx + 1 - 2 * side, head)
    z_next = (ctx + 2, head)
    z_prev = (ctx - 2, head)
    has_up = duo > 0
    has_down = duo < duos - 1
    own_count = pairs // 2
    x_halo = remote(x_ref.at[pl.ds(rows - RIM, RIM)], halo_x, hx_send, hx_recv, after)
    bc_halo = remote(bc_ref.at[pl.ds(rows - RIM, RIM)], halo_bc, hb_send, hb_recv, after)

    @pl.when(has_next)
    def _():
        bc_halo.start()
        x_halo.start()

    doc = doc_ref[0]
    dt = dt_ref[...]
    step = jnp.maximum(dt, 0.0) + jnp.log(1.0 + jnp.exp(-jnp.abs(dt)))
    head_id = lax.broadcasted_iota(jnp.int32, (heads, LANES), 0)
    logs = jnp.zeros((heads, LANES), F32)
    for h in range(heads):
        logs = jnp.where(head_id == h, alog_ref[h], logs)
    decay = jnp.exp(logs)[:, 0:1]
    r_id = lax.broadcasted_iota(jnp.int32, (rows, rows), 0)
    c_id = lax.broadcasted_iota(jnp.int32, (rows, rows), 1)
    same = (r_id >= doc) == (c_id >= doc)
    bias[...] = jnp.where(same & (r_id >= c_id), 0.0, -1e30)
    cum = exact_nn(-decay * step, jnp.where(r_id <= c_id, 1.0, 0.0))
    pos = lax.broadcasted_iota(jnp.int32, (heads, rows), 1)
    part = pos >= doc
    last_part = (rows - 1) >= doc
    enter = jnp.where(part, 0.0, jnp.exp(cum))
    final = cum[:, rows - 1 :]
    leave = jnp.where(part == last_part, jnp.exp(final - cum), 0.0)
    for k in range(pairs):
        pick = slice(2 * k, 2 * k + 2)
        stat[k, 0:2, :] = cum[pick]
        stat[k, 2:4, :] = step[pick]
        stat[k, 4:6, :] = leave[pick]
        stat[k, 6:8, :] = enter[pick]
    ends = jnp.where(doc >= rows, jnp.exp(final), 0.0)
    carry_own[...] = jnp.broadcast_to(ends, (heads, LANES))
    carry_copy = remote(carry_own, carry_oth, c_send, c_recv, partner)
    carry_copy.start()
    dgram[...] = jnp.zeros_like(dgram)

    @pl.when(has_next)
    def _():
        bc_halo.wait_send()
        x_halo.wait_send()

    @pl.when(has_prev)
    def _():
        bc_halo.wait_recv()
        x_halo.wait_recv()

    @pl.when(jnp.logical_not(has_prev))
    def _():
        halo_x[...] = jnp.zeros_like(halo_x)
        halo_bc[...] = jnp.zeros_like(halo_bc)

    @pl.when(jnp.logical_not(has_next))
    def _():
        nxt_x[...] = jnp.zeros_like(nxt_x)
        nxt_bc[...] = jnp.zeros_like(nxt_bc)

    @pl.when(jnp.logical_not(has_up))
    def _():
        z_in[...] = jnp.zeros_like(z_in)

    @pl.when(jnp.logical_not(has_down))
    def _():
        r_in[...] = jnp.zeros_like(r_in)

    def conv(pad_ref, weight):
        total = weight[0:1] * pad_ref[9 - taps : 9 - taps + rows, :]
        for tap in range(1, taps):
            at = 9 - taps + tap
            total = total + weight[tap : tap + 1] * pad_ref[at : at + rows, :]
        return total

    bcp[0:8, :] = halo_bc[RIM - 8 :, :].astype(F32)
    bcp[8:, :] = bc_ref[...].astype(F32)
    bc_pre = conv(bcp, wbc_ref[...].astype(F32))
    sig = sigmoid(bc_pre)
    bc_conv = (bc_pre * sig).astype(BF16)
    sgrad_bc[...] = sig * (1.0 + bc_pre * (1.0 - sig))
    b_mat[...] = bc_conv[:, :nstate]
    c_mat[...] = bc_conv[:, nstate:]
    gram[...] = dot_nt(bc_conv[:, nstate:], bc_conv[:, :nstate])

    lane = lax.broadcasted_iota(jnp.int32, (rows, LANES), 1)
    low = lane < half

    def spread(columns, at):
        return jnp.where(low, columns[:, at : at + 1], columns[:, at + 1 : at + 2])

    def prepare(k):
        cols = pl.ds(pl.multiple_of(k * LANES, LANES), LANES)
        turned = jnp.transpose(stat[k])
        step_k = spread(turned, 2)
        leave_k = spread(turned, 4)
        enter_k = spread(turned, 6)
        step_l[:, cols] = step_k
        leave_l[:, cols] = leave_k
        enter_l[:, cols] = enter_k
        xp[0:8, :] = halo_x[RIM - 8 :, cols].astype(F32)
        xp[8:, :] = x_ref[:, cols].astype(F32)
        pre = conv(xp, wx_ref[:, cols].astype(F32))
        sig_k = sigmoid(pre)
        sgrad[:, cols] = sig_k * (1.0 + pre * (1.0 - sig_k))
        xb = (pre * sig_k).astype(BF16)
        xc[:, cols] = xb
        xf = xb.astype(F32)
        sx[:, cols] = (xf * step_k).astype(BF16)
        lx_k = (xf * (leave_k * step_k)).astype(BF16)
        lx[:, cols] = lx_k
        edy_k = (dy_ref[:, cols].astype(F32) * enter_k).astype(BF16)
        edy[:, cols] = edy_k
        s_k = dot_tn(lx_k, b_mat[...])
        g_k = dot_tn(edy_k, c_mat[...])
        s_ref[k] = s_k
        g_ref[k] = g_k

        @pl.when(lax.rem(k, 2) != side)
        def _():
            s_out[k] = s_k.astype(BF16)
            remote(s_out.at[k], s_in.at[k], s_send.at[k], s_recv.at[k], partner).start()
            g_out[k] = g_k.astype(BF16)
            remote(g_out.at[k], g_in.at[k], g_send.at[k], g_recv.at[k], partner).start()

    def carry_rows(ref, k):
        return jnp.concatenate(
            [jnp.broadcast_to(ref[pl.ds(2 * k + j, 1), :], (half, LANES)) for j in range(2)], axis=0
        )

    def lag(kind, q):
        k = 2 * q + side
        own, other = carry_rows(carry_own, k), carry_rows(carry_oth, k)
        if kind == "z":
            remote(s_out.at[k], s_in.at[k], s_send.at[k], s_recv.at[k], partner).wait_recv()

            @pl.when(has_up)
            def _():
                remote(z_out.at[k], z_in.at[k], z_send.at[k], z_recv.at[k], z_next).wait_recv()

            mine, theirs, enters = s_ref[k], s_in[k].astype(F32), z_in[k].astype(F32)
            near = first
        else:
            remote(g_out.at[k], g_in.at[k], g_send.at[k], g_recv.at[k], partner).wait_recv()

            @pl.when(has_down)
            def _():
                remote(r_out.at[k], r_in.at[k], r_send.at[k], r_recv.at[k], z_prev).wait_recv()

            mine, theirs, enters = g_ref[k], g_in[k].astype(F32), r_in[k].astype(F32)
            near = jnp.logical_not(first)
        middle = jnp.where(near, own, other) * enters + jnp.where(near, mine, theirs)
        leaves = jnp.where(near, other, own) * middle + jnp.where(near, theirs, mine)
        keep = jnp.where(near, enters, middle).astype(BF16)
        give = jnp.where(near, middle, enters).astype(BF16)
        if kind == "z":

            @pl.when(has_down)
            def _():
                z_out[k] = leaves.astype(BF16)
                remote(z_out.at[k], z_in.at[k], z_send.at[k], z_recv.at[k], z_next).start()

            fin[k] = keep
            fout[k] = give
            remote(fout.at[k], fin.at[k], f_send.at[k], f_recv.at[k], partner).start()
        else:

            @pl.when(has_up)
            def _():
                r_out[k] = leaves.astype(BF16)
                remote(r_out.at[k], r_in.at[k], r_send.at[k], r_recv.at[k], z_prev).start()

            bin_[k] = keep
            bout[k] = give
            remote(bout.at[k], bin_.at[k], b_send.at[k], b_recv.at[k], partner).start()

    def chain(i):
        ahead = i - LAG * duo
        back = i - LAG * (duos - 1 - duo)

        @pl.when((ahead >= 0) & (ahead < own_count))
        def _():
            lag("z", ahead)

        @pl.when((back >= 0) & (back < own_count))
        def _():
            lag("r", back)

    def heavy(k):
        cols = pl.ds(pl.multiple_of(k * LANES, LANES), LANES)
        turned = jnp.transpose(stat[k])
        sx_k = sx[:, cols]
        dy_k = dy_ref[:, cols]
        zero = jnp.zeros_like(sx_k)
        outs, backs, weighs = [], [], []
        for j in range(2):
            mine = low if j == 0 else jnp.logical_not(low)
            ker = jnp.exp((turned[:, j : j + 1] - stat[k, j : j + 1, :]) + bias[...])
            mixing = (gram[...] * ker).astype(BF16)
            response = dot_nt(dy_k, jnp.where(mine, sx_k, zero))
            weighs.append(response * ker)
            outs.append(dot_nn(mixing, sx_k))
            backs.append(dot_tn(mixing, dy_k))
        dgram[...] += weighs[0] + weighs[1]
        intra[:, cols] = jnp.where(low, outs[0], outs[1])
        dsc[:, cols] = jnp.where(low, backs[0], backs[1])

    pl.loop(0, pairs)(prepare)
    carry_copy.wait_recv()

    @pl.loop(0, max(pairs, own_count + LAG * (duos - 1)))
    def _(i):
        chain(i)

        @pl.when(i < pairs)
        def _():
            heavy(i)

    gb_acc[...] = jnp.zeros_like(gb_acc)
    gc_acc[...] = jnp.zeros_like(gc_acc)

    def project(k):
        cols = pl.ds(pl.multiple_of(k * LANES, LANES), LANES)
        gc_acc[...] += dot_nn(edy[:, cols], fin[k])
        gb_acc[...] += dot_nn(lx[:, cols], bin_[k])

    @pl.loop(0, own_count)
    def _(q):
        project(2 * q + side)

    @pl.loop(0, own_count)
    def _(q):
        k = 2 * q + 1 - side
        remote(fout.at[k], fin.at[k], f_send.at[k], f_recv.at[k], partner).wait_recv()
        remote(bout.at[k], bin_.at[k], b_send.at[k], b_recv.at[k], partner).wait_recv()
        project(k)

    top, rest = halves(dgram[...])
    grad_c = gc_acc[...] + dot_nn(top, b_mat[...]) + dot_nn(rest, b_mat[...])
    grad_b = gb_acc[...] + dot_tn(top, c_mat[...]) + dot_tn(rest, c_mat[...])
    parts[head, :, 0:nstate] = grad_b.astype(BF16)
    parts[head, :, nstate:] = grad_c.astype(BF16)
    sends = []
    for off in range(1, n_head):
        to = (ctx, lax.rem(head + off, n_head))
        copy = remote(parts.at[head], parts.at[head], p_send.at[off - 1], p_recv.at[off - 1], to)
        copy.start()
        sends.append(copy)

    e_row = lax.broadcasted_iota(jnp.int32, (8, LANES), 0)
    e_col = lax.broadcasted_iota(jnp.int32, (8, LANES), 1) // half

    def finish(k):
        cols = pl.ds(pl.multiple_of(k * LANES, LANES), LANES)
        st = fin[k]
        ds = bin_[k]
        skip = jnp.where(low[0:1], dskip_ref[2 * k], dskip_ref[2 * k + 1])
        step_k = step_l[:, cols]
        leave_k = leave_l[:, cols]
        xf = xc[:, cols].astype(F32)
        dyf = dy_ref[:, cols].astype(F32)
        dsc_k = dsc[:, cols]
        y_all = intra[:, cols] + enter_l[:, cols] * dot_nt(c_mat[...], st)
        y_ref[:, cols] = (y_all + skip * xf).astype(BF16)
        dlv = leave_k * dot_nt(b_mat[...], ds)
        both = dsc_k + dlv
        gp[0:rows, cols] = (step_k * both + skip * dyf) * sgrad[:, cols]
        lterm = step_k * xf * dlv
        u1 = dyf * y_all - sx[:, cols].astype(F32) * dsc_k - lterm
        total = jnp.zeros((8, rows), F32)
        for at, value in ((0, u1), (2, xf * both), (4, lterm)):
            ones = jnp.where(e_row == e_col + at, 1.0, 0.0).astype(BF16)
            top, rest = halves(value)
            total = total + (dot_nt(ones, top) + dot_nt(ones, rest))
        rr[k] = total
        both_states = st.astype(F32) * ds.astype(F32) * carry_rows(carry_own, k)
        cs[k, 0:1, :] = jnp.sum(both_states[0:half], axis=0, keepdims=True)
        cs[k, 1:2, :] = jnp.sum(both_states[half:], axis=0, keepdims=True)

    pl.loop(0, pairs)(finish)

    x_rim = remote(gp.at[pl.ds(0, 8)], nxt_x, nx_send, nx_recv, before)

    @pl.when(has_prev)
    def _():
        x_rim.start()

    tri = jnp.where(r_id >= c_id, 1.0, 0.0)
    dt_sig = sigmoid(dt)
    pos2 = lax.broadcasted_iota(jnp.int32, (2, rows), 1) == rows - 1
    cums, direct = [], []
    for k in range(pairs):
        extra = jnp.sum(rr[k, 4:6, :], axis=1, keepdims=True) + jnp.sum(cs[k, 0:2, :], axis=1, keepdims=True)
        cums.append(rr[k, 0:2, :] + jnp.where(pos2, extra, 0.0))
        direct.append(rr[k, 2:4, :])
    d_log = exact_nn(jnp.concatenate(cums, axis=0), tri)
    gdt_ref[...] = (jnp.concatenate(direct, axis=0) - decay * d_log) * dt_sig

    @pl.when(has_next)
    def _():
        x_rim.wait_recv()

    gp[rows:, :] = nxt_x[...]

    @pl.loop(0, pairs)
    def _(k):
        cols = pl.ds(pl.multiple_of(k * LANES, LANES), LANES)
        weight = wx_ref[:, cols].astype(F32)
        total = weight[taps - 1 : taps] * gp[0:rows, cols]
        for off in range(1, taps):
            total = total + weight[taps - 1 - off : taps - off] * gp[off : off + rows, cols]
        gx_ref[:, cols] = total.astype(BF16)

    for off in range(1, n_head):
        source = lax.rem(head + n_head - off, n_head)
        remote(
            parts.at[source], parts.at[source], p_send.at[off - 1], p_recv.at[off - 1],
            (ctx, lax.rem(head + off, n_head)),
        ).wait_recv()
    total = parts[0].astype(F32)
    for other in range(1, n_head):
        total = total + parts[other].astype(F32)
    gbp[0:rows, :] = total * sgrad_bc[...]
    bc_rim = remote(gbp.at[pl.ds(0, 8)], nxt_bc, nb_send, nb_recv, before)

    @pl.when(has_prev)
    def _():
        bc_rim.start()

    for copy in sends:
        copy.wait_send()

    carry_copy.wait_send()

    @pl.loop(0, own_count)
    def _(q):
        k = 2 * q + side
        j = 2 * q + 1 - side
        remote(s_out.at[j], s_in.at[j], s_send.at[j], s_recv.at[j], partner).wait_send()
        remote(g_out.at[j], g_in.at[j], g_send.at[j], g_recv.at[j], partner).wait_send()
        remote(fout.at[k], fin.at[k], f_send.at[k], f_recv.at[k], partner).wait_send()
        remote(bout.at[k], bin_.at[k], b_send.at[k], b_recv.at[k], partner).wait_send()

        @pl.when(has_down)
        def _():
            remote(z_out.at[k], z_in.at[k], z_send.at[k], z_recv.at[k], z_next).wait_send()

        @pl.when(has_up)
        def _():
            remote(r_out.at[k], r_in.at[k], r_send.at[k], r_recv.at[k], z_prev).wait_send()

    @pl.when(has_next)
    def _():
        bc_rim.wait_recv()

    gbp[rows:, :] = nxt_bc[...]
    weight = wbc_ref[...].astype(F32)
    total = weight[taps - 1 : taps] * gbp[0:rows, :]
    for off in range(1, taps):
        total = total + weight[taps - 1 - off : taps - off] * gbp[off : off + rows, :]
    gbc_ref[...] = total.astype(BF16)

    @pl.when(has_prev)
    def _():
        x_rim.wait_send()
        bc_rim.wait_send()


def body(n_ctx, n_head, x_raw, bc_raw, conv_x_w, conv_bc_w, dt_raw, a_log, d_skip, doc_starts, grad_y):
    rows, channels = x_raw.shape
    heads = a_log.shape[0]
    nstate = bc_raw.shape[1] // 2
    pairs = channels // LANES
    vmem = pl.BlockSpec(memory_space=pltpu.VMEM)
    smem = pl.BlockSpec(memory_space=pltpu.SMEM)
    wide = pltpu.VMEM((rows, channels), F32)
    wide_h = pltpu.VMEM((rows, channels), BF16)
    state = pltpu.VMEM((pairs, LANES, nstate), F32)
    state_h = pltpu.VMEM((pairs, LANES, nstate), BF16)
    dma = pltpu.SemaphoreType.DMA
    scratch = [
        pltpu.VMEM((RIM, channels), BF16),
        pltpu.VMEM((RIM, 2 * nstate), BF16),
        pltpu.VMEM((rows + 8, LANES), F32),
        pltpu.VMEM((rows + 8, 2 * nstate), F32),
        pltpu.VMEM((pairs, 8, rows), F32),
        state, state,
        pltpu.VMEM((heads, LANES), F32),
        pltpu.VMEM((heads, LANES), F32),
        state_h, state_h, state_h, state_h, state_h, state_h, state_h, state_h, state_h, state_h, state_h, state_h,
        wide_h, wide_h, wide_h, wide_h,
        wide, wide, wide, wide, wide, wide,
        pltpu.VMEM((rows + 8, channels), F32),
        pltpu.VMEM((rows + 8, 2 * nstate), F32),
        pltpu.VMEM((rows, 2 * nstate), F32),
        pltpu.VMEM((rows, nstate), BF16),
        pltpu.VMEM((rows, nstate), BF16),
        pltpu.VMEM((rows, rows), F32),
        pltpu.VMEM((rows, rows), F32),
        pltpu.VMEM((rows, rows), F32),
        pltpu.VMEM((rows, nstate), F32),
        pltpu.VMEM((rows, nstate), F32),
        pltpu.VMEM((pairs, 8, rows), F32),
        pltpu.VMEM((pairs, 8, LANES), F32),
        pltpu.VMEM((n_head, rows, 2 * nstate), BF16),
        pltpu.VMEM((8, channels), F32),
        pltpu.VMEM((8, 2 * nstate), F32),
        dma, dma, dma, dma,
        dma((pairs,)), dma((pairs,)), dma((pairs,)), dma((pairs,)), dma, dma,
        dma((pairs,)), dma((pairs,)), dma((pairs,)), dma((pairs,)),
        dma((pairs,)), dma((pairs,)), dma((pairs,)), dma((pairs,)),
        dma((n_head - 1,)), dma((n_head - 1,)),
        dma, dma, dma, dma,
    ]
    return pl.pallas_call(
        functools.partial(kernel, n_ctx, n_head, pairs),
        out_shape=(
            jax.ShapeDtypeStruct((rows, channels), BF16),
            jax.ShapeDtypeStruct((rows, channels), BF16),
            jax.ShapeDtypeStruct((rows, 2 * nstate), BF16),
            jax.ShapeDtypeStruct((heads, rows), F32),
        ),
        in_specs=[vmem] * 5 + [smem, smem, smem, vmem],
        out_specs=(vmem, vmem, vmem, vmem),
        scratch_shapes=scratch,
        compiler_params=pltpu.CompilerParams(
            collective_id=0, has_side_effects=True, vmem_limit_bytes=56 * 1024 * 1024
        ),
        cost_estimate=pl.CostEstimate(flops=3 * 10**9, bytes_accessed=6 * 2**20, transcendentals=3 * 10**6),
    )(
        x_raw, bc_raw, conv_x_w, conv_bc_w, dt_raw, a_log, d_skip, doc_starts, grad_y
    )


def solution(mesh):
    in_specs = (
        P("ctx", "head"),
        P("ctx", None),
        P(None, "head"),
        P(),
        P("head", "ctx"),
        P("head"),
        P("head"),
        P("ctx"),
        P("ctx", "head"),
    )
    out_specs = (P("ctx", "head"), P("ctx", "head"), P("ctx", None), P("head", "ctx"))
    inner = functools.partial(body, mesh.shape["ctx"], mesh.shape["head"])
    return jax.shard_map(inner, mesh=mesh, in_specs=in_specs, out_specs=out_specs, check_vma=False)
```

```python
import functools

import jax
import jax.numpy as jnp
from jax import lax
from jax.experimental import pallas as pl
from jax.experimental.pallas import tpu as pltpu
from jax.sharding import PartitionSpec as P

F32 = jnp.float32
BF16 = jnp.bfloat16
LANES = 128
RIM = 16
LAG = 2
PIECES = 4


def dot_nn(a, b):
    return lax.dot_general(a, b, (((1,), (0,)), ((), ())), preferred_element_type=F32)


def dot_nt(a, b):
    return lax.dot_general(a, b, (((1,), (1,)), ((), ())), preferred_element_type=F32)


def dot_tn(a, b):
    return lax.dot_general(a, b, (((0,), (0,)), ((), ())), preferred_element_type=F32)


def exact_nn(a, b):
    return lax.dot_general(
        a, b, (((1,), (0,)), ((), ())), precision=lax.Precision.HIGHEST, preferred_element_type=F32
    )


def halves(value):
    top = value.astype(BF16)
    return top, (value - top.astype(F32)).astype(BF16)


def sigmoid(v):
    return 0.5 + 0.5 * jnp.tanh(0.5 * v)


def kernel(
    n_ctx, n_head, pairs,
    x_ref, bc_ref, wx_ref, wbc_ref, dt_ref, alog_ref, dskip_ref, doc_ref, dy_ref,
    y_ref, gx_ref, gbc_ref, gdt_ref,
    halo_x, halo_bc, xp, bcp, stat, s_ref, g_ref, carry_own, carry_oth,
    s_out, s_in, g_out, g_in, fin, fout, bin_, bout, z_in, z_out, r_in, r_out,
    xc, sx, lx, edy, sgrad, intra, dsc, step_l, leave_l, enter_l, gp, gbp, sgrad_bc,
    b_mat, c_mat, gram, bias, dgram, gb_acc, gc_acc, rr, cs, parts, nxt_x, nxt_bc,
    hx_send, hx_recv, hb_send, hb_recv, f_send, f_recv, b_send, b_recv, c_send, c_recv,
    s_send, s_recv, g_send, g_recv, z_send, z_recv, r_send, r_recv,
    p_send, p_recv, nx_send, nx_recv, nb_send, nb_recv,
):
    rows = x_ref.shape[0]
    heads = dt_ref.shape[0]
    nstate = bc_ref.shape[1] // 2
    taps = wx_ref.shape[0]
    ctx = lax.axis_index("ctx")
    head = lax.axis_index("head")
    has_prev = ctx > 0
    has_next = ctx < n_ctx - 1
    half = LANES // 2
    mid = rows // 2

    barrier = pltpu.get_barrier_semaphore()

    for dist in (1, 2):
        for sign in (-1, 1):

            @pl.when((ctx + sign * dist >= 0) & (ctx + sign * dist < n_ctx))
            def _(dist=dist, sign=sign):
                pl.semaphore_signal(
                    barrier, inc=1, device_id=(ctx + sign * dist, head), device_id_type=pl.DeviceIdType.MESH
                )

    for off in range(1, n_head):
        pl.semaphore_signal(
            barrier, inc=1, device_id=(ctx, lax.rem(head + off, n_head)), device_id_type=pl.DeviceIdType.MESH
        )

    for lows in range(3):
        for highs in range(3):
            is_low = ctx == lows if lows < 2 else ctx >= 2
            left = n_ctx - 1 - ctx
            is_high = left == highs if highs < 2 else left >= 2

            @pl.when(is_low & is_high)
            def _(count=lows + highs + n_head - 1):
                pl.semaphore_wait(barrier, count)

    def remote(src, dst, send, recv, to):
        return pltpu.make_async_remote_copy(
            src_ref=src, dst_ref=dst, send_sem=send, recv_sem=recv, device_id=to,
            device_id_type=pl.DeviceIdType.MESH,
        )

    after = (ctx + 1, head)
    before = (ctx - 1, head)
    side = lax.rem(ctx, 2)
    first = side == 0
    duo = ctx // 2
    duos = n_ctx // 2
    partner = (ctx + 1 - 2 * side, head)
    z_next = (ctx + 2, head)
    z_prev = (ctx - 2, head)
    has_up = duo > 0
    has_down = duo < duos - 1
    own_count = pairs // 2
    x_halo = remote(x_ref.at[pl.ds(rows - RIM, RIM)], halo_x, hx_send, hx_recv, after)
    bc_halo = remote(bc_ref.at[pl.ds(rows - RIM, RIM)], halo_bc, hb_send, hb_recv, after)

    @pl.when(has_next)
    def _():
        bc_halo.start()
        x_halo.start()

    doc = doc_ref[0]
    dt = dt_ref[...]
    step = jnp.maximum(dt, 0.0) + jnp.log(1.0 + jnp.exp(-jnp.abs(dt)))
    head_id = lax.broadcasted_iota(jnp.int32, (heads, LANES), 0)
    logs = jnp.zeros((heads, LANES), F32)
    for h in range(heads):
        logs = jnp.where(head_id == h, alog_ref[h], logs)
    decay = jnp.exp(logs)[:, 0:1]
    r_id = lax.broadcasted_iota(jnp.int32, (rows, rows), 0)
    c_id = lax.broadcasted_iota(jnp.int32, (rows, rows), 1)
    same = (r_id >= doc) == (c_id >= doc)
    bias[...] = jnp.where(same & (r_id >= c_id), 0.0, -1e30)
    cum = exact_nn(-decay * step, jnp.where(r_id <= c_id, 1.0, 0.0))
    pos = lax.broadcasted_iota(jnp.int32, (heads, rows), 1)
    part = pos >= doc
    last_part = (rows - 1) >= doc
    enter = jnp.where(part, 0.0, jnp.exp(cum))
    final = cum[:, rows - 1 :]
    leave = jnp.where(part == last_part, jnp.exp(final - cum), 0.0)
    for k in range(pairs):
        pick = slice(2 * k, 2 * k + 2)
        stat[k, 0:2, :] = cum[pick]
        stat[k, 2:4, :] = step[pick]
        stat[k, 4:6, :] = leave[pick]
        stat[k, 6:8, :] = enter[pick]
    ends = jnp.where(doc >= rows, jnp.exp(final), 0.0)
    carry_own[...] = jnp.broadcast_to(ends, (heads, LANES))
    carry_copy = remote(carry_own, carry_oth, c_send, c_recv, partner)
    carry_copy.start()
    dgram[...] = jnp.zeros_like(dgram)

    @pl.when(has_next)
    def _():
        bc_halo.wait_send()
        x_halo.wait_send()

    @pl.when(has_prev)
    def _():
        bc_halo.wait_recv()
        x_halo.wait_recv()

    @pl.when(jnp.logical_not(has_prev))
    def _():
        halo_x[...] = jnp.zeros_like(halo_x)
        halo_bc[...] = jnp.zeros_like(halo_bc)

    @pl.when(jnp.logical_not(has_next))
    def _():
        nxt_x[...] = jnp.zeros_like(nxt_x)
        nxt_bc[...] = jnp.zeros_like(nxt_bc)

    @pl.when(jnp.logical_not(has_up))
    def _():
        z_in[...] = jnp.zeros_like(z_in)

    @pl.when(jnp.logical_not(has_down))
    def _():
        r_in[...] = jnp.zeros_like(r_in)

    def conv(pad_ref, weight):
        total = weight[0:1] * pad_ref[9 - taps : 9 - taps + rows, :]
        for tap in range(1, taps):
            at = 9 - taps + tap
            total = total + weight[tap : tap + 1] * pad_ref[at : at + rows, :]
        return total

    bcp[0:8, :] = halo_bc[RIM - 8 :, :].astype(F32)
    bcp[8:, :] = bc_ref[...].astype(F32)
    bc_pre = conv(bcp, wbc_ref[...].astype(F32))
    sig = sigmoid(bc_pre)
    bc_conv = (bc_pre * sig).astype(BF16)
    sgrad_bc[...] = sig * (1.0 + bc_pre * (1.0 - sig))
    b_mat[...] = bc_conv[:, :nstate]
    c_mat[...] = bc_conv[:, nstate:]
    gram[...] = dot_nt(bc_conv[:, nstate:], bc_conv[:, :nstate])

    lane = lax.broadcasted_iota(jnp.int32, (rows, LANES), 1)
    low = lane < half

    def spread(columns, at):
        return jnp.where(low, columns[:, at : at + 1], columns[:, at + 1 : at + 2])

    def prepare(k, slot):
        cols = pl.ds(pl.multiple_of(k * LANES, LANES), LANES)
        turned = jnp.transpose(stat[k])
        step_k = spread(turned, 2)
        leave_k = spread(turned, 4)
        enter_k = spread(turned, 6)
        step_l[:, cols] = step_k
        leave_l[:, cols] = leave_k
        enter_l[:, cols] = enter_k
        xp_k = xp.at[slot]
        xp_k[0:8, :] = halo_x[RIM - 8 :, cols].astype(F32)
        xp_k[8:, :] = x_ref[:, cols].astype(F32)
        pre = conv(xp_k, wx_ref[:, cols].astype(F32))
        sig_k = sigmoid(pre)
        sgrad[:, cols] = sig_k * (1.0 + pre * (1.0 - sig_k))
        xb = (pre * sig_k).astype(BF16)
        xc[:, cols] = xb
        xf = xb.astype(F32)
        sx[:, cols] = (xf * step_k).astype(BF16)
        lx_k = (xf * (leave_k * step_k)).astype(BF16)
        lx[:, cols] = lx_k
        edy_k = (dy_ref[:, cols].astype(F32) * enter_k).astype(BF16)
        edy[:, cols] = edy_k
        s_k = dot_tn(lx_k, b_mat[...])
        g_k = dot_tn(edy_k, c_mat[...])
        s_ref[k] = s_k
        g_ref[k] = g_k

        @pl.when(lax.rem(k, 2) != side)
        def _():
            s_out[k] = s_k.astype(BF16)
            remote(s_out.at[k], s_in.at[k], s_send.at[k], s_recv.at[k], partner).start()
            g_out[k] = g_k.astype(BF16)
            remote(g_out.at[k], g_in.at[k], g_send.at[k], g_recv.at[k], partner).start()

    def carry_rows(ref, k):
        return jnp.concatenate(
            [jnp.broadcast_to(ref[pl.ds(2 * k + j, 1), :], (half, LANES)) for j in range(2)], axis=0
        )

    def lag(kind, q):
        k = 2 * q + side
        own, other = carry_rows(carry_own, k), carry_rows(carry_oth, k)
        if kind == "z":
            remote(s_out.at[k], s_in.at[k], s_send.at[k], s_recv.at[k], partner).wait_recv()

            @pl.when(has_up)
            def _():
                remote(z_out.at[k], z_in.at[k], z_send.at[k], z_recv.at[k], z_next).wait_recv()

            mine, theirs, enters = s_ref[k], s_in[k].astype(F32), z_in[k].astype(F32)
            near = first
        else:
            remote(g_out.at[k], g_in.at[k], g_send.at[k], g_recv.at[k], partner).wait_recv()

            @pl.when(has_down)
            def _():
                remote(r_out.at[k], r_in.at[k], r_send.at[k], r_recv.at[k], z_prev).wait_recv()

            mine, theirs, enters = g_ref[k], g_in[k].astype(F32), r_in[k].astype(F32)
            near = jnp.logical_not(first)
        middle = jnp.where(near, own, other) * enters + jnp.where(near, mine, theirs)
        leaves = jnp.where(near, other, own) * middle + jnp.where(near, theirs, mine)
        keep = jnp.where(near, enters, middle).astype(BF16)
        give = jnp.where(near, middle, enters).astype(BF16)
        if kind == "z":

            @pl.when(has_down)
            def _():
                z_out[k] = leaves.astype(BF16)
                remote(z_out.at[k], z_in.at[k], z_send.at[k], z_recv.at[k], z_next).start()

            fin[k] = keep
            fout[k] = give
            remote(fout.at[k], fin.at[k], f_send.at[k], f_recv.at[k], partner).start()
        else:

            @pl.when(has_up)
            def _():
                r_out[k] = leaves.astype(BF16)
                remote(r_out.at[k], r_in.at[k], r_send.at[k], r_recv.at[k], z_prev).start()

            bin_[k] = keep
            bout[k] = give
            remote(bout.at[k], bin_.at[k], b_send.at[k], b_recv.at[k], partner).start()

    def chain(i):
        ahead = i - LAG * duo
        back = i - LAG * (duos - 1 - duo)

        @pl.when((ahead >= 0) & (ahead < own_count))
        def _():
            lag("z", ahead)

        @pl.when((back >= 0) & (back < own_count))
        def _():
            lag("r", back)

    def heavy(k):
        cols = pl.ds(pl.multiple_of(k * LANES, LANES), LANES)
        turned = jnp.transpose(stat[k])
        sx_k = sx[:, cols]
        dy_k = dy_ref[:, cols]
        zero = jnp.zeros_like(sx_k)
        outs, backs, weighs = [], [], []
        for j in range(2):
            mine = low if j == 0 else jnp.logical_not(low)
            sx_j = jnp.where(mine, sx_k, zero)
            column, row = turned[:, j : j + 1], stat[k, j : j + 1, :]
            sources = []
            for at, width in ((0, mid), (mid, rows)):
                ker = jnp.exp((column[at : at + mid] - row[:, :width]) + bias[at : at + mid, :width])
                mixing = (gram[at : at + mid, :width] * ker).astype(BF16)
                weighs.append(dot_nt(dy_k[at : at + mid], sx_j[:width]) * ker)
                outs.append(dot_nn(mixing, sx_k[:width]))
                sources.append(dot_tn(mixing, dy_k[at : at + mid]))
            backs.append((sources[1][:mid] + sources[0], sources[1][mid:]))
        dgram[0:mid, 0:mid] += weighs[0] + weighs[2]
        dgram[mid:, :] += weighs[1] + weighs[3]
        for h in range(2):
            rows_h = slice(h * mid, (h + 1) * mid)
            intra[rows_h, cols] = jnp.where(low[:mid], outs[h], outs[2 + h])
            dsc[rows_h, cols] = jnp.where(low[:mid], backs[0][h], backs[1][h])

    @pl.loop(0, pairs // 2)
    def _(k):
        prepare(2 * k, 0)
        prepare(2 * k + 1, 1)

    carry_copy.wait_recv()

    @pl.loop(0, max(pairs, own_count + LAG * (duos - 1)))
    def _(i):
        chain(i)

        @pl.when(i < pairs)
        def _():
            heavy(i)

    gb_acc[...] = jnp.zeros_like(gb_acc)
    gc_acc[...] = jnp.zeros_like(gc_acc)

    def project(k):
        cols = pl.ds(pl.multiple_of(k * LANES, LANES), LANES)
        gc_acc[...] += dot_nn(edy[:, cols], fin[k])
        gb_acc[...] += dot_nn(lx[:, cols], bin_[k])

    @pl.loop(0, own_count)
    def _(q):
        project(2 * q + side)

    @pl.loop(0, own_count)
    def _(q):
        k = 2 * q + 1 - side
        remote(fout.at[k], fin.at[k], f_send.at[k], f_recv.at[k], partner).wait_recv()
        remote(bout.at[k], bin_.at[k], b_send.at[k], b_recv.at[k], partner).wait_recv()
        project(k)

    top, rest = halves(dgram[...])
    grad_c = gc_acc[...] + dot_nn(top, b_mat[...]) + dot_nn(rest, b_mat[...])
    grad_b = gb_acc[...] + dot_tn(top, c_mat[...]) + dot_tn(rest, c_mat[...])
    parts[head, :, 0:nstate] = grad_b.astype(BF16)
    parts[head, :, nstate:] = grad_c.astype(BF16)
    sends = []
    for off in range(1, n_head):
        to = (ctx, lax.rem(head + off, n_head))
        copy = remote(parts.at[head], parts.at[head], p_send.at[off - 1], p_recv.at[off - 1], to)
        copy.start()
        sends.append(copy)

    e_row = lax.broadcasted_iota(jnp.int32, (3 * LANES, LANES), 0)
    e_col = lax.broadcasted_iota(jnp.int32, (3 * LANES, LANES), 1)
    e_at = (e_row % LANES) // half + jnp.where(e_row < 2 * LANES, 0, heads) - e_col
    rr[...] = jnp.zeros_like(rr)

    def finish(k):
        cols = pl.ds(pl.multiple_of(k * LANES, LANES), LANES)
        st = fin[k]
        ds = bin_[k]
        skip = jnp.where(low[0:1], dskip_ref[2 * k], dskip_ref[2 * k + 1])
        step_k = step_l[:, cols]
        leave_k = leave_l[:, cols]
        xf = xc[:, cols].astype(F32)
        dyf = dy_ref[:, cols].astype(F32)
        dsc_k = dsc[:, cols]
        y_all = intra[:, cols] + enter_l[:, cols] * dot_nt(c_mat[...], st)
        y_ref[:, cols] = (y_all + skip * xf).astype(BF16)
        dlv = leave_k * dot_nt(b_mat[...], ds)
        both = dsc_k + dlv
        gp[0:rows, cols] = (step_k * both + skip * dyf) * sgrad[:, cols]
        lterm = step_k * xf * dlv
        u1 = dyf * y_all - sx[:, cols].astype(F32) * dsc_k - lterm
        top, rest = halves(u1)
        ones = jnp.where(e_at == -2 * k, 1.0, 0.0).astype(BF16)
        sums = dot_nn(jnp.concatenate([top, rest, (xf * both).astype(BF16)], axis=1), ones)
        lsum = jnp.sum(lterm, axis=0, keepdims=True)
        both_states = st.astype(F32) * ds.astype(F32) * carry_rows(carry_own, k)
        for j in range(2):
            mine = low[0:1] if j == 0 else jnp.logical_not(low[0:1])
            cs[k, j : j + 1, :] = jnp.where(mine, lsum, 0.0) + jnp.sum(
                both_states[j * half : (j + 1) * half], axis=0, keepdims=True
            )
        return sums

    @pl.loop(0, pairs // 2)
    def _(k):
        rr[...] += finish(2 * k) + finish(2 * k + 1)

    x_rim = remote(gp.at[pl.ds(0, 8)], nxt_x, nx_send, nx_recv, before)

    @pl.when(has_prev)
    def _():
        x_rim.start()

    for off in range(1, n_head):
        source = lax.rem(head + n_head - off, n_head)
        remote(
            parts.at[source], parts.at[source], p_send.at[off - 1], p_recv.at[off - 1],
            (ctx, lax.rem(head + off, n_head)),
        ).wait_recv()
    total = parts[0].astype(F32)
    for other in range(1, n_head):
        total = total + parts[other].astype(F32)
    gbp[0:rows, :] = total * sgrad_bc[...]
    bc_rim = remote(gbp.at[pl.ds(0, 8)], nxt_bc, nb_send, nb_recv, before)

    @pl.when(has_prev)
    def _():
        bc_rim.start()

    tri = jnp.where(r_id >= c_id, 1.0, 0.0)
    turned_sums = jnp.transpose(rr[...])
    extra = jnp.concatenate([cs[k, 0:2, :] for k in range(pairs)], axis=0)
    extra = jnp.sum(extra, axis=1, keepdims=True)
    d_log = exact_nn(turned_sums[:heads] + jnp.where(pos == rows - 1, extra, 0.0), tri)
    gdt_ref[...] = (turned_sums[heads : 2 * heads] - decay * d_log) * sigmoid(dt)

    @pl.when(has_next)
    def _():
        x_rim.wait_recv()

    gp[rows:, :] = nxt_x[...]

    @pl.loop(0, pairs)
    def _(k):
        cols = pl.ds(pl.multiple_of(k * LANES, LANES), LANES)
        weight = wx_ref[:, cols].astype(F32)
        total = weight[taps - 1 : taps] * gp[0:rows, cols]
        for off in range(1, taps):
            total = total + weight[taps - 1 - off : taps - off] * gp[off : off + rows, cols]
        gx_ref[:, cols] = total.astype(BF16)

    for copy in sends:
        copy.wait_send()

    carry_copy.wait_send()

    @pl.loop(0, own_count)
    def _(q):
        k = 2 * q + side
        j = 2 * q + 1 - side
        remote(s_out.at[j], s_in.at[j], s_send.at[j], s_recv.at[j], partner).wait_send()
        remote(g_out.at[j], g_in.at[j], g_send.at[j], g_recv.at[j], partner).wait_send()
        remote(fout.at[k], fin.at[k], f_send.at[k], f_recv.at[k], partner).wait_send()
        remote(bout.at[k], bin_.at[k], b_send.at[k], b_recv.at[k], partner).wait_send()

        @pl.when(has_down)
        def _():
            remote(z_out.at[k], z_in.at[k], z_send.at[k], z_recv.at[k], z_next).wait_send()

        @pl.when(has_up)
        def _():
            remote(r_out.at[k], r_in.at[k], r_send.at[k], r_recv.at[k], z_prev).wait_send()

    @pl.when(has_next)
    def _():
        bc_rim.wait_recv()

    gbp[rows:, :] = nxt_bc[...]
    weight = wbc_ref[...].astype(F32)
    total = weight[taps - 1 : taps] * gbp[0:rows, :]
    for off in range(1, taps):
        total = total + weight[taps - 1 - off : taps - off] * gbp[off : off + rows, :]
    gbc_ref[...] = total.astype(BF16)

    @pl.when(has_prev)
    def _():
        x_rim.wait_send()
        bc_rim.wait_send()


def hand_over(*refs):
    count = (len(refs) - 1) // 2
    sems = refs[-1]
    copies = []
    for at in range(count):
        source, target = refs[at], refs[count + at]
        total = source.shape[0]
        pieces = PIECES if total % (PIECES * RIM) == 0 else 1
        size = total // pieces
        for piece in range(pieces):
            rows = pl.ds(piece * size, size)
            copies.append(
                pltpu.make_async_copy(source.at[rows], target.at[rows], sems.at[len(copies)])
            )
    for copy in copies:
        copy.start()
    for copy in copies:
        copy.wait()


def body(n_ctx, n_head, x_raw, bc_raw, conv_x_w, conv_bc_w, dt_raw, a_log, d_skip, doc_starts, grad_y):
    rows, channels = x_raw.shape
    heads = a_log.shape[0]
    nstate = bc_raw.shape[1] // 2
    pairs = channels // LANES
    vmem = pl.BlockSpec(memory_space=pltpu.VMEM)
    smem = pl.BlockSpec(memory_space=pltpu.SMEM)
    wide = pltpu.VMEM((rows, channels), F32)
    wide_h = pltpu.VMEM((rows, channels), BF16)
    state = pltpu.VMEM((pairs, LANES, nstate), F32)
    state_h = pltpu.VMEM((pairs, LANES, nstate), BF16)
    dma = pltpu.SemaphoreType.DMA
    scratch = [
        pltpu.VMEM((RIM, channels), BF16),
        pltpu.VMEM((RIM, 2 * nstate), BF16),
        pltpu.VMEM((2, rows + 8, LANES), F32),
        pltpu.VMEM((rows + 8, 2 * nstate), F32),
        pltpu.VMEM((pairs, 8, rows), F32),
        state, state,
        pltpu.VMEM((heads, LANES), F32),
        pltpu.VMEM((heads, LANES), F32),
        state_h, state_h, state_h, state_h, state_h, state_h, state_h, state_h, state_h, state_h, state_h, state_h,
        wide_h, wide_h, wide_h, wide_h,
        wide, wide, wide, wide, wide, wide,
        pltpu.VMEM((rows + 8, channels), F32),
        pltpu.VMEM((rows + 8, 2 * nstate), F32),
        pltpu.VMEM((rows, 2 * nstate), F32),
        pltpu.VMEM((rows, nstate), BF16),
        pltpu.VMEM((rows, nstate), BF16),
        pltpu.VMEM((rows, rows), F32),
        pltpu.VMEM((rows, rows), F32),
        pltpu.VMEM((rows, rows), F32),
        pltpu.VMEM((rows, nstate), F32),
        pltpu.VMEM((rows, nstate), F32),
        pltpu.VMEM((rows, LANES), F32),
        pltpu.VMEM((pairs, 8, LANES), F32),
        pltpu.VMEM((n_head, rows, 2 * nstate), BF16),
        pltpu.VMEM((8, channels), F32),
        pltpu.VMEM((8, 2 * nstate), F32),
        dma, dma, dma, dma,
        dma((pairs,)), dma((pairs,)), dma((pairs,)), dma((pairs,)), dma, dma,
        dma((pairs,)), dma((pairs,)), dma((pairs,)), dma((pairs,)),
        dma((pairs,)), dma((pairs,)), dma((pairs,)), dma((pairs,)),
        dma((n_head - 1,)), dma((n_head - 1,)),
        dma, dma, dma, dma,
    ]
    shapes = (
        jax.ShapeDtypeStruct((rows, channels), BF16),
        jax.ShapeDtypeStruct((rows, channels), BF16),
        jax.ShapeDtypeStruct((rows, 2 * nstate), BF16),
        jax.ShapeDtypeStruct((heads, rows), F32),
    )
    results = pl.pallas_call(
        functools.partial(kernel, n_ctx, n_head, pairs),
        out_shape=shapes,
        in_specs=[vmem] * 5 + [smem, smem, smem, vmem],
        out_specs=(vmem, vmem, vmem, vmem),
        scratch_shapes=scratch,
        compiler_params=pltpu.CompilerParams(
            collective_id=0, has_side_effects=True, vmem_limit_bytes=56 * 1024 * 1024
        ),
        cost_estimate=pl.CostEstimate(flops=3 * 10**9, bytes_accessed=6 * 2**20, transcendentals=3 * 10**6),
    )(
        x_raw, bc_raw, conv_x_w, conv_bc_w, dt_raw, a_log, d_skip, doc_starts, grad_y
    )
    anywhere = pl.BlockSpec(memory_space=pl.ANY)
    return pl.pallas_call(
        hand_over,
        out_shape=shapes,
        in_specs=[pl.BlockSpec(memory_space=pltpu.HBM)] * 4,
        out_specs=(anywhere,) * 4,
        scratch_shapes=[dma((4 * PIECES,))],
    )(*results)


def solution(mesh):
    in_specs = (
        P("ctx", "head"),
        P("ctx", None),
        P(None, "head"),
        P(),
        P("head", "ctx"),
        P("head"),
        P("head"),
        P("ctx"),
        P("ctx", "head"),
    )
    out_specs = (P("ctx", "head"), P("ctx", "head"), P("ctx", None), P("head", "ctx"))
    inner = functools.partial(body, mesh.shape["ctx"], mesh.shape["head"])
    return jax.shard_map(inner, mesh=mesh, in_specs=in_specs, out_specs=out_specs, check_vma=False)
```

```python
import functools

import jax
import jax.numpy as jnp
from jax import lax
from jax.experimental import pallas as pl
from jax.experimental.pallas import tpu as pltpu
from jax.sharding import PartitionSpec as P

F32 = jnp.float32
BF16 = jnp.bfloat16
LANES = 128
RIM = 16
LAG = 3
PIECES = 4


def dot_nn(a, b):
    return lax.dot_general(a, b, (((1,), (0,)), ((), ())), preferred_element_type=F32)


def dot_nt(a, b):
    return lax.dot_general(a, b, (((1,), (1,)), ((), ())), preferred_element_type=F32)


def dot_tn(a, b):
    return lax.dot_general(a, b, (((0,), (0,)), ((), ())), preferred_element_type=F32)


def exact_nn(a, b):
    return lax.dot_general(
        a, b, (((1,), (0,)), ((), ())), precision=lax.Precision.HIGHEST, preferred_element_type=F32
    )


def halves(value):
    top = value.astype(BF16)
    return top, (value - top.astype(F32)).astype(BF16)


def sigmoid(v):
    return 0.5 + 0.5 * jnp.tanh(0.5 * v)


def kernel(
    n_ctx, n_head, pairs,
    x_ref, bc_ref, wx_ref, wbc_ref, dt_ref, alog_ref, dskip_ref, doc_ref, dy_ref,
    y_ref, gx_ref, gbc_ref, gdt_ref,
    halo_x, halo_bc, xp, bcp, stat, s_ref, g_ref, carry_own, carry_oth,
    s_out, s_in, g_out, g_in, fin, fout, bin_, bout, z_in, z_out, r_in, r_out,
    xc, sx, lx, edy, sgrad, intra, dsc, step_l, leave_l, enter_l, gp, gbp, sgrad_bc,
    b_mat, c_mat, gram, bias, dgram, gb_acc, gc_acc, rr, cs, parts, nxt_x, nxt_bc,
    hx_send, hx_recv, hb_send, hb_recv, f_send, f_recv, b_send, b_recv, c_send, c_recv,
    s_send, s_recv, g_send, g_recv, z_send, z_recv, r_send, r_recv,
    p_send, p_recv, nx_send, nx_recv, nb_send, nb_recv,
):
    rows = x_ref.shape[0]
    heads = dt_ref.shape[0]
    nstate = bc_ref.shape[1] // 2
    taps = wx_ref.shape[0]
    ctx = lax.axis_index("ctx")
    head = lax.axis_index("head")
    has_prev = ctx > 0
    has_next = ctx < n_ctx - 1
    half = LANES // 2
    mid = rows // 2

    barrier = pltpu.get_barrier_semaphore()

    for dist in (1, 2):
        for sign in (-1, 1):

            @pl.when((ctx + sign * dist >= 0) & (ctx + sign * dist < n_ctx))
            def _(dist=dist, sign=sign):
                pl.semaphore_signal(
                    barrier, inc=1, device_id=(ctx + sign * dist, head), device_id_type=pl.DeviceIdType.MESH
                )

    for off in range(1, n_head):
        pl.semaphore_signal(
            barrier, inc=1, device_id=(ctx, lax.rem(head + off, n_head)), device_id_type=pl.DeviceIdType.MESH
        )

    for lows in range(3):
        for highs in range(3):
            is_low = ctx == lows if lows < 2 else ctx >= 2
            left = n_ctx - 1 - ctx
            is_high = left == highs if highs < 2 else left >= 2

            @pl.when(is_low & is_high)
            def _(count=lows + highs + n_head - 1):
                pl.semaphore_wait(barrier, count)

    def remote(src, dst, send, recv, to):
        return pltpu.make_async_remote_copy(
            src_ref=src, dst_ref=dst, send_sem=send, recv_sem=recv, device_id=to,
            device_id_type=pl.DeviceIdType.MESH,
        )

    after = (ctx + 1, head)
    before = (ctx - 1, head)
    side = lax.rem(ctx, 2)
    first = side == 0
    duo = ctx // 2
    duos = n_ctx // 2
    partner = (ctx + 1 - 2 * side, head)
    z_next = (ctx + 2, head)
    z_prev = (ctx - 2, head)
    has_up = duo > 0
    has_down = duo < duos - 1
    own_count = pairs // 2
    x_halo = remote(x_ref.at[pl.ds(rows - RIM, RIM)], halo_x, hx_send, hx_recv, after)
    bc_halo = remote(bc_ref.at[pl.ds(rows - RIM, RIM)], halo_bc, hb_send, hb_recv, after)

    @pl.when(has_next)
    def _():
        bc_halo.start()
        x_halo.start()

    doc = doc_ref[0]
    dt = dt_ref[...]
    step = jnp.maximum(dt, 0.0) + jnp.log(1.0 + jnp.exp(-jnp.abs(dt)))
    head_id = lax.broadcasted_iota(jnp.int32, (heads, LANES), 0)
    logs = jnp.zeros((heads, LANES), F32)
    for h in range(heads):
        logs = jnp.where(head_id == h, alog_ref[h], logs)
    decay = jnp.exp(logs)[:, 0:1]
    r_id = lax.broadcasted_iota(jnp.int32, (rows, rows), 0)
    c_id = lax.broadcasted_iota(jnp.int32, (rows, rows), 1)
    same = (r_id >= doc) == (c_id >= doc)
    bias[...] = jnp.where(same & (r_id >= c_id), 0.0, -1e30)
    cum = exact_nn(-decay * step, jnp.where(r_id <= c_id, 1.0, 0.0))
    pos = lax.broadcasted_iota(jnp.int32, (heads, rows), 1)
    part = pos >= doc
    last_part = (rows - 1) >= doc
    enter = jnp.where(part, 0.0, jnp.exp(cum))
    final = cum[:, rows - 1 :]
    leave = jnp.where(part == last_part, jnp.exp(final - cum), 0.0)
    for k in range(pairs):
        pick = slice(2 * k, 2 * k + 2)
        stat[k, 0:2, :] = cum[pick]
        stat[k, 2:4, :] = step[pick]
        stat[k, 4:6, :] = leave[pick]
        stat[k, 6:8, :] = enter[pick]
    ends = jnp.where(doc >= rows, jnp.exp(final), 0.0)
    carry_own[...] = jnp.broadcast_to(ends, (heads, LANES))
    carry_copy = remote(carry_own, carry_oth, c_send, c_recv, partner)
    carry_copy.start()
    dgram[...] = jnp.zeros_like(dgram)

    @pl.when(has_next)
    def _():
        bc_halo.wait_send()
        x_halo.wait_send()

    @pl.when(has_prev)
    def _():
        bc_halo.wait_recv()
        x_halo.wait_recv()

    @pl.when(jnp.logical_not(has_prev))
    def _():
        halo_x[...] = jnp.zeros_like(halo_x)
        halo_bc[...] = jnp.zeros_like(halo_bc)

    @pl.when(jnp.logical_not(has_next))
    def _():
        nxt_x[...] = jnp.zeros_like(nxt_x)
        nxt_bc[...] = jnp.zeros_like(nxt_bc)

    @pl.when(jnp.logical_not(has_up))
    def _():
        z_in[...] = jnp.zeros_like(z_in)

    @pl.when(jnp.logical_not(has_down))
    def _():
        r_in[...] = jnp.zeros_like(r_in)

    def conv(pad_ref, weight):
        total = weight[0:1] * pad_ref[9 - taps : 9 - taps + rows, :]
        for tap in range(1, taps):
            at = 9 - taps + tap
            total = total + weight[tap : tap + 1] * pad_ref[at : at + rows, :]
        return total

    bcp[0:8, :] = halo_bc[RIM - 8 :, :].astype(F32)
    bcp[8:, :] = bc_ref[...].astype(F32)
    bc_pre = conv(bcp, wbc_ref[...].astype(F32))
    sig = sigmoid(bc_pre)
    bc_conv = (bc_pre * sig).astype(BF16)
    sgrad_bc[...] = sig * (1.0 + bc_pre * (1.0 - sig))
    b_mat[...] = bc_conv[:, :nstate]
    c_mat[...] = bc_conv[:, nstate:]
    gram[...] = dot_nt(bc_conv[:, nstate:], bc_conv[:, :nstate])

    lane = lax.broadcasted_iota(jnp.int32, (rows, LANES), 1)
    low = lane < half

    def spread(columns, at):
        return jnp.where(low, columns[:, at : at + 1], columns[:, at + 1 : at + 2])

    def prepare(k, slot):
        cols = pl.ds(pl.multiple_of(k * LANES, LANES), LANES)
        turned = jnp.transpose(stat[k])
        step_k = spread(turned, 2)
        leave_k = spread(turned, 4)
        enter_k = spread(turned, 6)
        step_l[:, cols] = step_k
        leave_l[:, cols] = leave_k
        enter_l[:, cols] = enter_k
        xp_k = xp.at[slot]
        xp_k[0:8, :] = halo_x[RIM - 8 :, cols].astype(F32)
        xp_k[8:, :] = x_ref[:, cols].astype(F32)
        pre = conv(xp_k, wx_ref[:, cols].astype(F32))
        sig_k = sigmoid(pre)
        sgrad[:, cols] = sig_k * (1.0 + pre * (1.0 - sig_k))
        xb = (pre * sig_k).astype(BF16)
        xc[:, cols] = xb
        xf = xb.astype(F32)
        sx[:, cols] = (xf * step_k).astype(BF16)
        lx_k = (xf * (leave_k * step_k)).astype(BF16)
        lx[:, cols] = lx_k
        edy_k = (dy_ref[:, cols].astype(F32) * enter_k).astype(BF16)
        edy[:, cols] = edy_k
        s_k = dot_tn(lx_k, b_mat[...])
        g_k = dot_tn(edy_k, c_mat[...])
        s_ref[k] = s_k
        g_ref[k] = g_k

        @pl.when(lax.rem(k, 2) != side)
        def _():
            s_out[k] = s_k.astype(BF16)
            remote(s_out.at[k], s_in.at[k], s_send.at[k], s_recv.at[k], partner).start()
            g_out[k] = g_k.astype(BF16)
            remote(g_out.at[k], g_in.at[k], g_send.at[k], g_recv.at[k], partner).start()

    def carry_rows(ref, k):
        return jnp.concatenate(
            [jnp.broadcast_to(ref[pl.ds(2 * k + j, 1), :], (half, LANES)) for j in range(2)], axis=0
        )

    def lag(kind, q):
        k = 2 * q + side
        own, other = carry_rows(carry_own, k), carry_rows(carry_oth, k)
        if kind == "z":
            remote(s_out.at[k], s_in.at[k], s_send.at[k], s_recv.at[k], partner).wait_recv()

            @pl.when(has_up)
            def _():
                remote(z_out.at[k], z_in.at[k], z_send.at[k], z_recv.at[k], z_next).wait_recv()

            mine, theirs, enters = s_ref[k], s_in[k].astype(F32), z_in[k].astype(F32)
            near = first
        else:
            remote(g_out.at[k], g_in.at[k], g_send.at[k], g_recv.at[k], partner).wait_recv()

            @pl.when(has_down)
            def _():
                remote(r_out.at[k], r_in.at[k], r_send.at[k], r_recv.at[k], z_prev).wait_recv()

            mine, theirs, enters = g_ref[k], g_in[k].astype(F32), r_in[k].astype(F32)
            near = jnp.logical_not(first)
        middle = jnp.where(near, own, other) * enters + jnp.where(near, mine, theirs)
        leaves = jnp.where(near, other, own) * middle + jnp.where(near, theirs, mine)
        keep = jnp.where(near, enters, middle).astype(BF16)
        give = jnp.where(near, middle, enters).astype(BF16)
        if kind == "z":

            @pl.when(has_down)
            def _():
                z_out[k] = leaves.astype(BF16)
                remote(z_out.at[k], z_in.at[k], z_send.at[k], z_recv.at[k], z_next).start()

            fin[k] = keep
            fout[k] = give
            remote(fout.at[k], fin.at[k], f_send.at[k], f_recv.at[k], partner).start()
        else:

            @pl.when(has_up)
            def _():
                r_out[k] = leaves.astype(BF16)
                remote(r_out.at[k], r_in.at[k], r_send.at[k], r_recv.at[k], z_prev).start()

            bin_[k] = keep
            bout[k] = give
            remote(bout.at[k], bin_.at[k], b_send.at[k], b_recv.at[k], partner).start()

    def chain(i):
        ahead = i - LAG * duo
        back = i - LAG * (duos - 1 - duo)

        @pl.when((ahead >= 0) & (ahead < own_count))
        def _():
            lag("z", ahead)

        @pl.when((back >= 0) & (back < own_count))
        def _():
            lag("r", back)

    def heavy(k):
        cols = pl.ds(pl.multiple_of(k * LANES, LANES), LANES)
        turned = jnp.transpose(stat[k])
        sx_k = sx[:, cols]
        dy_k = dy_ref[:, cols]
        zero = jnp.zeros_like(sx_k)
        outs, backs, weighs = [], [], []
        for j in range(2):
            mine = low if j == 0 else jnp.logical_not(low)
            sx_j = jnp.where(mine, sx_k, zero)
            column, row = turned[:, j : j + 1], stat[k, j : j + 1, :]
            sources = []
            for at, width in ((0, mid), (mid, rows)):
                ker = jnp.exp((column[at : at + mid] - row[:, :width]) + bias[at : at + mid, :width])
                mixing = (gram[at : at + mid, :width] * ker).astype(BF16)
                weighs.append(dot_nt(dy_k[at : at + mid], sx_j[:width]) * ker)
                outs.append(dot_nn(mixing, sx_k[:width]))
                sources.append(dot_tn(mixing, dy_k[at : at + mid]))
            backs.append((sources[1][:mid] + sources[0], sources[1][mid:]))
        dgram[0:mid, 0:mid] += weighs[0] + weighs[2]
        dgram[mid:, :] += weighs[1] + weighs[3]
        for h in range(2):
            rows_h = slice(h * mid, (h + 1) * mid)
            intra[rows_h, cols] = jnp.where(low[:mid], outs[h], outs[2 + h])
            dsc[rows_h, cols] = jnp.where(low[:mid], backs[0][h], backs[1][h])

    @pl.loop(0, pairs // 2)
    def _(k):
        late = k // (pairs // 4)
        at = 4 * (k % (pairs // 4)) + jnp.where(late == 0, 1 - side, side)
        prepare(at, 0)
        prepare(at + 2, 1)

    carry_copy.wait_recv()

    @pl.loop(0, max(pairs, own_count + LAG * (duos - 1)))
    def _(i):
        chain(i)

        @pl.when(i < pairs)
        def _():
            heavy(i)

    gb_acc[...] = jnp.zeros_like(gb_acc)
    gc_acc[...] = jnp.zeros_like(gc_acc)

    def project(k):
        cols = pl.ds(pl.multiple_of(k * LANES, LANES), LANES)
        gc_acc[...] += dot_nn(edy[:, cols], fin[k])
        gb_acc[...] += dot_nn(lx[:, cols], bin_[k])

    @pl.loop(0, own_count)
    def _(q):
        project(2 * q + side)

    @pl.loop(0, own_count)
    def _(q):
        k = 2 * q + 1 - side
        remote(fout.at[k], fin.at[k], f_send.at[k], f_recv.at[k], partner).wait_recv()
        remote(bout.at[k], bin_.at[k], b_send.at[k], b_recv.at[k], partner).wait_recv()
        project(k)

    top, rest = halves(dgram[...])
    grad_c = gc_acc[...] + dot_nn(top, b_mat[...]) + dot_nn(rest, b_mat[...])
    grad_b = gb_acc[...] + dot_tn(top, c_mat[...]) + dot_tn(rest, c_mat[...])
    parts[head, :, 0:nstate] = grad_b.astype(BF16)
    parts[head, :, nstate:] = grad_c.astype(BF16)
    sends = []
    for off in range(1, n_head):
        to = (ctx, lax.rem(head + off, n_head))
        copy = remote(parts.at[head], parts.at[head], p_send.at[off - 1], p_recv.at[off - 1], to)
        copy.start()
        sends.append(copy)

    e_row = lax.broadcasted_iota(jnp.int32, (3 * LANES, LANES), 0)
    e_col = lax.broadcasted_iota(jnp.int32, (3 * LANES, LANES), 1)
    e_at = (e_row % LANES) // half + jnp.where(e_row < 2 * LANES, 0, heads) - e_col
    rr[...] = jnp.zeros_like(rr)

    def finish(k):
        cols = pl.ds(pl.multiple_of(k * LANES, LANES), LANES)
        st = fin[k]
        ds = bin_[k]
        skip = jnp.where(low[0:1], dskip_ref[2 * k], dskip_ref[2 * k + 1])
        step_k = step_l[:, cols]
        leave_k = leave_l[:, cols]
        xf = xc[:, cols].astype(F32)
        dyf = dy_ref[:, cols].astype(F32)
        dsc_k = dsc[:, cols]
        y_all = intra[:, cols] + enter_l[:, cols] * dot_nt(c_mat[...], st)
        y_ref[:, cols] = (y_all + skip * xf).astype(BF16)
        dlv = leave_k * dot_nt(b_mat[...], ds)
        both = dsc_k + dlv
        gp[0:rows, cols] = (step_k * both + skip * dyf) * sgrad[:, cols]
        lterm = step_k * xf * dlv
        u1 = dyf * y_all - sx[:, cols].astype(F32) * dsc_k - lterm
        top, rest = halves(u1)
        ones = jnp.where(e_at == -2 * k, 1.0, 0.0).astype(BF16)
        sums = dot_nn(jnp.concatenate([top, rest, (xf * both).astype(BF16)], axis=1), ones)
        lsum = jnp.sum(lterm, axis=0, keepdims=True)
        both_states = st.astype(F32) * ds.astype(F32) * carry_rows(carry_own, k)
        for j in range(2):
            mine = low[0:1] if j == 0 else jnp.logical_not(low[0:1])
            cs[k, j : j + 1, :] = jnp.where(mine, lsum, 0.0) + jnp.sum(
                both_states[j * half : (j + 1) * half], axis=0, keepdims=True
            )
        return sums

    @pl.loop(0, pairs // 2)
    def _(k):
        rr[...] += finish(2 * k) + finish(2 * k + 1)

    x_rim = remote(gp.at[pl.ds(0, 8)], nxt_x, nx_send, nx_recv, before)

    @pl.when(has_prev)
    def _():
        x_rim.start()

    for off in range(1, n_head):
        source = lax.rem(head + n_head - off, n_head)
        remote(
            parts.at[source], parts.at[source], p_send.at[off - 1], p_recv.at[off - 1],
            (ctx, lax.rem(head + off, n_head)),
        ).wait_recv()
    total = parts[0].astype(F32)
    for other in range(1, n_head):
        total = total + parts[other].astype(F32)
    gbp[0:rows, :] = total * sgrad_bc[...]
    bc_rim = remote(gbp.at[pl.ds(0, 8)], nxt_bc, nb_send, nb_recv, before)

    @pl.when(has_prev)
    def _():
        bc_rim.start()

    tri = jnp.where(r_id >= c_id, 1.0, 0.0)
    turned_sums = jnp.transpose(rr[...])
    extra = jnp.concatenate([cs[k, 0:2, :] for k in range(pairs)], axis=0)
    extra = jnp.sum(extra, axis=1, keepdims=True)
    d_log = exact_nn(turned_sums[:heads] + jnp.where(pos == rows - 1, extra, 0.0), tri)
    gdt_ref[...] = (turned_sums[heads : 2 * heads] - decay * d_log) * sigmoid(dt)

    @pl.when(has_next)
    def _():
        x_rim.wait_recv()

    gp[rows:, :] = nxt_x[...]

    @pl.loop(0, pairs)
    def _(k):
        cols = pl.ds(pl.multiple_of(k * LANES, LANES), LANES)
        weight = wx_ref[:, cols].astype(F32)
        total = weight[taps - 1 : taps] * gp[0:rows, cols]
        for off in range(1, taps):
            total = total + weight[taps - 1 - off : taps - off] * gp[off : off + rows, cols]
        gx_ref[:, cols] = total.astype(BF16)

    for copy in sends:
        copy.wait_send()

    carry_copy.wait_send()

    @pl.loop(0, own_count)
    def _(q):
        k = 2 * q + side
        j = 2 * q + 1 - side
        remote(s_out.at[j], s_in.at[j], s_send.at[j], s_recv.at[j], partner).wait_send()
        remote(g_out.at[j], g_in.at[j], g_send.at[j], g_recv.at[j], partner).wait_send()
        remote(fout.at[k], fin.at[k], f_send.at[k], f_recv.at[k], partner).wait_send()
        remote(bout.at[k], bin_.at[k], b_send.at[k], b_recv.at[k], partner).wait_send()

        @pl.when(has_down)
        def _():
            remote(z_out.at[k], z_in.at[k], z_send.at[k], z_recv.at[k], z_next).wait_send()

        @pl.when(has_up)
        def _():
            remote(r_out.at[k], r_in.at[k], r_send.at[k], r_recv.at[k], z_prev).wait_send()

    @pl.when(has_next)
    def _():
        bc_rim.wait_recv()

    gbp[rows:, :] = nxt_bc[...]
    weight = wbc_ref[...].astype(F32)
    total = weight[taps - 1 : taps] * gbp[0:rows, :]
    for off in range(1, taps):
        total = total + weight[taps - 1 - off : taps - off] * gbp[off : off + rows, :]
    gbc_ref[...] = total.astype(BF16)

    @pl.when(has_prev)
    def _():
        x_rim.wait_send()
        bc_rim.wait_send()


def hand_over(*refs):
    count = len(refs) // 2
    for at in range(count):
        refs[count + at][...] = refs[at][...]


def body(n_ctx, n_head, x_raw, bc_raw, conv_x_w, conv_bc_w, dt_raw, a_log, d_skip, doc_starts, grad_y):
    rows, channels = x_raw.shape
    heads = a_log.shape[0]
    nstate = bc_raw.shape[1] // 2
    pairs = channels // LANES
    vmem = pl.BlockSpec(memory_space=pltpu.VMEM)
    smem = pl.BlockSpec(memory_space=pltpu.SMEM)
    wide = pltpu.VMEM((rows, channels), F32)
    wide_h = pltpu.VMEM((rows, channels), BF16)
    state = pltpu.VMEM((pairs, LANES, nstate), F32)
    state_h = pltpu.VMEM((pairs, LANES, nstate), BF16)
    dma = pltpu.SemaphoreType.DMA
    scratch = [
        pltpu.VMEM((RIM, channels), BF16),
        pltpu.VMEM((RIM, 2 * nstate), BF16),
        pltpu.VMEM((2, rows + 8, LANES), F32),
        pltpu.VMEM((rows + 8, 2 * nstate), F32),
        pltpu.VMEM((pairs, 8, rows), F32),
        state, state,
        pltpu.VMEM((heads, LANES), F32),
        pltpu.VMEM((heads, LANES), F32),
        state_h, state_h, state_h, state_h, state_h, state_h, state_h, state_h, state_h, state_h, state_h, state_h,
        wide_h, wide_h, wide_h, wide_h,
        wide, wide, wide, wide, wide, wide,
        pltpu.VMEM((rows + 8, channels), F32),
        pltpu.VMEM((rows + 8, 2 * nstate), F32),
        pltpu.VMEM((rows, 2 * nstate), F32),
        pltpu.VMEM((rows, nstate), BF16),
        pltpu.VMEM((rows, nstate), BF16),
        pltpu.VMEM((rows, rows), F32),
        pltpu.VMEM((rows, rows), F32),
        pltpu.VMEM((rows, rows), F32),
        pltpu.VMEM((rows, nstate), F32),
        pltpu.VMEM((rows, nstate), F32),
        pltpu.VMEM((rows, LANES), F32),
        pltpu.VMEM((pairs, 8, LANES), F32),
        pltpu.VMEM((n_head, rows, 2 * nstate), BF16),
        pltpu.VMEM((8, channels), F32),
        pltpu.VMEM((8, 2 * nstate), F32),
        dma, dma, dma, dma,
        dma((pairs,)), dma((pairs,)), dma((pairs,)), dma((pairs,)), dma, dma,
        dma((pairs,)), dma((pairs,)), dma((pairs,)), dma((pairs,)),
        dma((pairs,)), dma((pairs,)), dma((pairs,)), dma((pairs,)),
        dma((n_head - 1,)), dma((n_head - 1,)),
        dma, dma, dma, dma,
    ]
    shapes = (
        jax.ShapeDtypeStruct((rows, channels), BF16),
        jax.ShapeDtypeStruct((rows, channels), BF16),
        jax.ShapeDtypeStruct((rows, 2 * nstate), BF16),
        jax.ShapeDtypeStruct((heads, rows), F32),
    )
    results = pl.pallas_call(
        functools.partial(kernel, n_ctx, n_head, pairs),
        out_shape=shapes,
        in_specs=[vmem] * 5 + [smem, smem, smem, vmem],
        out_specs=(vmem, vmem, vmem, vmem),
        scratch_shapes=scratch,
        compiler_params=pltpu.CompilerParams(
            collective_id=0, has_side_effects=True, vmem_limit_bytes=56 * 1024 * 1024
        ),
        cost_estimate=pl.CostEstimate(flops=3 * 10**9, bytes_accessed=6 * 2**20, transcendentals=3 * 10**6),
    )(
        x_raw, bc_raw, conv_x_w, conv_bc_w, dt_raw, a_log, d_skip, doc_starts, grad_y
    )
    blocks = [
        pl.BlockSpec((rows // PIECES, channels), lambda i: (i, 0)),
        pl.BlockSpec((rows // PIECES, channels), lambda i: (i, 0)),
        pl.BlockSpec((rows // PIECES, 2 * nstate), lambda i: (i, 0)),
        pl.BlockSpec((heads, rows), lambda i: (0, 0)),
    ]
    return pl.pallas_call(
        hand_over, grid=(PIECES,), out_shape=shapes, in_specs=blocks, out_specs=tuple(blocks)
    )(*results)


def solution(mesh):
    in_specs = (
        P("ctx", "head"),
        P("ctx", None),
        P(None, "head"),
        P(),
        P("head", "ctx"),
        P("head"),
        P("head"),
        P("ctx"),
        P("ctx", "head"),
    )
    out_specs = (P("ctx", "head"), P("ctx", "head"), P("ctx", None), P("head", "ctx"))
    inner = functools.partial(body, mesh.shape["ctx"], mesh.shape["head"])
    return jax.shard_map(inner, mesh=mesh, in_specs=in_specs, out_specs=out_specs, check_vma=False)
```

```python
import functools

import jax
import jax.numpy as jnp
from jax import lax
from jax.experimental import pallas as pl
from jax.experimental.pallas import tpu as pltpu
from jax.sharding import PartitionSpec as P

F32 = jnp.float32
BF16 = jnp.bfloat16
LANES = 128
RIM = 16
LAG = 3
PIECES = 4


def dot_nn(a, b):
    return lax.dot_general(a, b, (((1,), (0,)), ((), ())), preferred_element_type=F32)


def dot_nt(a, b):
    return lax.dot_general(a, b, (((1,), (1,)), ((), ())), preferred_element_type=F32)


def dot_tn(a, b):
    return lax.dot_general(a, b, (((0,), (0,)), ((), ())), preferred_element_type=F32)


def exact_nn(a, b):
    return lax.dot_general(
        a, b, (((1,), (0,)), ((), ())), precision=lax.Precision.HIGHEST, preferred_element_type=F32
    )


def halves(value):
    top = value.astype(BF16)
    return top, (value - top.astype(F32)).astype(BF16)


def sigmoid(v):
    return 0.5 + 0.5 * jnp.tanh(0.5 * v)


def kernel(
    n_ctx, n_head, pairs,
    x_ref, bc_ref, wx_ref, wbc_ref, dt_ref, alog_ref, dskip_ref, doc_ref, dy_ref,
    y_ref, gx_ref, gbc_ref, gdt_ref,
    halo_x, halo_bc, xp, bcp, stat, s_ref, g_ref, carry_own, carry_oth,
    s_out, s_in, g_out, g_in, fin, fout, bin_, bout, z_in, z_out, r_in, r_out,
    xc, sx, lx, edy, sgrad, intra, dsc, step_l, leave_l, enter_l, gp, gbp, sgrad_bc,
    b_mat, c_mat, gram, bias, dgram, gb_acc, gc_acc, rr, cs, parts, whole_part, summed, nxt_x, nxt_bc,
    hx_send, hx_recv, hb_send, hb_recv, f_send, f_recv, b_send, b_recv, c_send, c_recv,
    s_send, s_recv, g_send, g_recv, z_send, z_recv, r_send, r_recv,
    p_send, p_recv, q_send, q_recv, nx_send, nx_recv, nb_send, nb_recv,
):
    rows = x_ref.shape[0]
    heads = dt_ref.shape[0]
    nstate = bc_ref.shape[1] // 2
    taps = wx_ref.shape[0]
    ctx = lax.axis_index("ctx")
    head = lax.axis_index("head")
    has_prev = ctx > 0
    has_next = ctx < n_ctx - 1
    half = LANES // 2
    mid = rows // 2

    barrier = pltpu.get_barrier_semaphore()

    for dist in (1, 2):
        for sign in (-1, 1):

            @pl.when((ctx + sign * dist >= 0) & (ctx + sign * dist < n_ctx))
            def _(dist=dist, sign=sign):
                pl.semaphore_signal(
                    barrier, inc=1, device_id=(ctx + sign * dist, head), device_id_type=pl.DeviceIdType.MESH
                )

    for off in range(1, n_head):
        pl.semaphore_signal(
            barrier, inc=1, device_id=(ctx, lax.rem(head + off, n_head)), device_id_type=pl.DeviceIdType.MESH
        )

    for lows in range(3):
        for highs in range(3):
            is_low = ctx == lows if lows < 2 else ctx >= 2
            left = n_ctx - 1 - ctx
            is_high = left == highs if highs < 2 else left >= 2

            @pl.when(is_low & is_high)
            def _(count=lows + highs + n_head - 1):
                pl.semaphore_wait(barrier, count)

    def remote(src, dst, send, recv, to):
        return pltpu.make_async_remote_copy(
            src_ref=src, dst_ref=dst, send_sem=send, recv_sem=recv, device_id=to,
            device_id_type=pl.DeviceIdType.MESH,
        )

    after = (ctx + 1, head)
    before = (ctx - 1, head)
    side = lax.rem(ctx, 2)
    first = side == 0
    duo = ctx // 2
    duos = n_ctx // 2
    partner = (ctx + 1 - 2 * side, head)
    z_next = (ctx + 2, head)
    z_prev = (ctx - 2, head)
    has_up = duo > 0
    has_down = duo < duos - 1
    own_count = pairs // 2
    x_halo = remote(x_ref.at[pl.ds(rows - RIM, RIM)], halo_x, hx_send, hx_recv, after)
    bc_halo = remote(bc_ref.at[pl.ds(rows - RIM, RIM)], halo_bc, hb_send, hb_recv, after)

    @pl.when(has_next)
    def _():
        bc_halo.start()
        x_halo.start()

    doc = doc_ref[0]
    dt = dt_ref[...]
    step = jnp.maximum(dt, 0.0) + jnp.log(1.0 + jnp.exp(-jnp.abs(dt)))
    head_id = lax.broadcasted_iota(jnp.int32, (heads, LANES), 0)
    logs = jnp.zeros((heads, LANES), F32)
    for h in range(heads):
        logs = jnp.where(head_id == h, alog_ref[h], logs)
    decay = jnp.exp(logs)[:, 0:1]
    r_id = lax.broadcasted_iota(jnp.int32, (rows, rows), 0)
    c_id = lax.broadcasted_iota(jnp.int32, (rows, rows), 1)
    same = (r_id >= doc) == (c_id >= doc)
    bias[...] = jnp.where(same & (r_id >= c_id), 0.0, -1e30)
    cum = exact_nn(-decay * step, jnp.where(r_id <= c_id, 1.0, 0.0))
    pos = lax.broadcasted_iota(jnp.int32, (heads, rows), 1)
    part = pos >= doc
    last_part = (rows - 1) >= doc
    enter = jnp.where(part, 0.0, jnp.exp(cum))
    final = cum[:, rows - 1 :]
    leave = jnp.where(part == last_part, jnp.exp(final - cum), 0.0)
    for k in range(pairs):
        pick = slice(2 * k, 2 * k + 2)
        stat[k, 0:2, :] = cum[pick]
        stat[k, 2:4, :] = step[pick]
        stat[k, 4:6, :] = leave[pick]
        stat[k, 6:8, :] = enter[pick]
    ends = jnp.where(doc >= rows, jnp.exp(final), 0.0)
    carry_own[...] = jnp.broadcast_to(ends, (heads, LANES))
    carry_copy = remote(carry_own, carry_oth, c_send, c_recv, partner)
    carry_copy.start()
    dgram[...] = jnp.zeros_like(dgram)

    @pl.when(has_next)
    def _():
        bc_halo.wait_send()
        x_halo.wait_send()

    @pl.when(has_prev)
    def _():
        bc_halo.wait_recv()
        x_halo.wait_recv()

    @pl.when(jnp.logical_not(has_prev))
    def _():
        halo_x[...] = jnp.zeros_like(halo_x)
        halo_bc[...] = jnp.zeros_like(halo_bc)

    @pl.when(jnp.logical_not(has_next))
    def _():
        nxt_x[...] = jnp.zeros_like(nxt_x)
        nxt_bc[...] = jnp.zeros_like(nxt_bc)

    @pl.when(jnp.logical_not(has_up))
    def _():
        z_in[...] = jnp.zeros_like(z_in)

    @pl.when(jnp.logical_not(has_down))
    def _():
        r_in[...] = jnp.zeros_like(r_in)

    def conv(pad_ref, weight):
        total = weight[0:1] * pad_ref[9 - taps : 9 - taps + rows, :]
        for tap in range(1, taps):
            at = 9 - taps + tap
            total = total + weight[tap : tap + 1] * pad_ref[at : at + rows, :]
        return total

    bcp[0:8, :] = halo_bc[RIM - 8 :, :].astype(F32)
    bcp[8:, :] = bc_ref[...].astype(F32)
    bc_pre = conv(bcp, wbc_ref[...].astype(F32))
    sig = sigmoid(bc_pre)
    bc_conv = (bc_pre * sig).astype(BF16)
    sgrad_bc[...] = sig * (1.0 + bc_pre * (1.0 - sig))
    b_mat[...] = bc_conv[:, :nstate]
    c_mat[...] = bc_conv[:, nstate:]
    gram[...] = dot_nt(bc_conv[:, nstate:], bc_conv[:, :nstate])

    lane = lax.broadcasted_iota(jnp.int32, (rows, LANES), 1)
    low = lane < half

    def spread(columns, at):
        return jnp.where(low, columns[:, at : at + 1], columns[:, at + 1 : at + 2])

    def prepare(k, slot):
        cols = pl.ds(pl.multiple_of(k * LANES, LANES), LANES)
        turned = jnp.transpose(stat[k])
        step_k = spread(turned, 2)
        leave_k = spread(turned, 4)
        enter_k = spread(turned, 6)
        step_l[:, cols] = step_k
        leave_l[:, cols] = leave_k
        enter_l[:, cols] = enter_k
        xp_k = xp.at[slot]
        xp_k[0:8, :] = halo_x[RIM - 8 :, cols].astype(F32)
        xp_k[8:, :] = x_ref[:, cols].astype(F32)
        pre = conv(xp_k, wx_ref[:, cols].astype(F32))
        sig_k = sigmoid(pre)
        sgrad[:, cols] = sig_k * (1.0 + pre * (1.0 - sig_k))
        xb = (pre * sig_k).astype(BF16)
        xc[:, cols] = xb
        xf = xb.astype(F32)
        sx[:, cols] = (xf * step_k).astype(BF16)
        lx_k = (xf * (leave_k * step_k)).astype(BF16)
        lx[:, cols] = lx_k
        edy_k = (dy_ref[:, cols].astype(F32) * enter_k).astype(BF16)
        edy[:, cols] = edy_k
        s_k = dot_tn(lx_k, b_mat[...])
        g_k = dot_tn(edy_k, c_mat[...])
        s_ref[k] = s_k
        g_ref[k] = g_k

        @pl.when(lax.rem(k, 2) != side)
        def _():
            s_out[k] = s_k.astype(BF16)
            remote(s_out.at[k], s_in.at[k], s_send.at[k], s_recv.at[k], partner).start()
            g_out[k] = g_k.astype(BF16)
            remote(g_out.at[k], g_in.at[k], g_send.at[k], g_recv.at[k], partner).start()

    def carry_rows(ref, k):
        return jnp.concatenate(
            [jnp.broadcast_to(ref[pl.ds(2 * k + j, 1), :], (half, LANES)) for j in range(2)], axis=0
        )

    def lag(kind, q):
        k = 2 * q + side
        own, other = carry_rows(carry_own, k), carry_rows(carry_oth, k)
        if kind == "z":
            remote(s_out.at[k], s_in.at[k], s_send.at[k], s_recv.at[k], partner).wait_recv()

            @pl.when(has_up)
            def _():
                remote(z_out.at[k], z_in.at[k], z_send.at[k], z_recv.at[k], z_next).wait_recv()

            mine, theirs, enters = s_ref[k], s_in[k].astype(F32), z_in[k].astype(F32)
            near = first
        else:
            remote(g_out.at[k], g_in.at[k], g_send.at[k], g_recv.at[k], partner).wait_recv()

            @pl.when(has_down)
            def _():
                remote(r_out.at[k], r_in.at[k], r_send.at[k], r_recv.at[k], z_prev).wait_recv()

            mine, theirs, enters = g_ref[k], g_in[k].astype(F32), r_in[k].astype(F32)
            near = jnp.logical_not(first)
        middle = jnp.where(near, own, other) * enters + jnp.where(near, mine, theirs)
        leaves = jnp.where(near, other, own) * middle + jnp.where(near, theirs, mine)
        keep = jnp.where(near, enters, middle).astype(BF16)
        give = jnp.where(near, middle, enters).astype(BF16)
        if kind == "z":

            @pl.when(has_down)
            def _():
                z_out[k] = leaves.astype(BF16)
                remote(z_out.at[k], z_in.at[k], z_send.at[k], z_recv.at[k], z_next).start()

            fin[k] = keep
            fout[k] = give
            remote(fout.at[k], fin.at[k], f_send.at[k], f_recv.at[k], partner).start()
        else:

            @pl.when(has_up)
            def _():
                r_out[k] = leaves.astype(BF16)
                remote(r_out.at[k], r_in.at[k], r_send.at[k], r_recv.at[k], z_prev).start()

            bin_[k] = keep
            bout[k] = give
            remote(bout.at[k], bin_.at[k], b_send.at[k], b_recv.at[k], partner).start()

    def chain(i):
        ahead = i - LAG * duo
        back = i - LAG * (duos - 1 - duo)

        @pl.when((ahead >= 0) & (ahead < own_count))
        def _():
            lag("z", ahead)

        @pl.when((back >= 0) & (back < own_count))
        def _():
            lag("r", back)

    def heavy(k):
        cols = pl.ds(pl.multiple_of(k * LANES, LANES), LANES)
        turned = jnp.transpose(stat[k])
        sx_k = sx[:, cols]
        dy_k = dy_ref[:, cols]
        zero = jnp.zeros_like(sx_k)
        outs, backs, weighs = [], [], []
        for j in range(2):
            mine = low if j == 0 else jnp.logical_not(low)
            sx_j = jnp.where(mine, sx_k, zero)
            column, row = turned[:, j : j + 1], stat[k, j : j + 1, :]
            sources = []
            for at, width in ((0, mid), (mid, rows)):
                ker = jnp.exp((column[at : at + mid] - row[:, :width]) + bias[at : at + mid, :width])
                mixing = (gram[at : at + mid, :width] * ker).astype(BF16)
                weighs.append(dot_nt(dy_k[at : at + mid], sx_j[:width]) * ker)
                outs.append(dot_nn(mixing, sx_k[:width]))
                sources.append(dot_tn(mixing, dy_k[at : at + mid]))
            backs.append((sources[1][:mid] + sources[0], sources[1][mid:]))
        dgram[0:mid, 0:mid] += weighs[0] + weighs[2]
        dgram[mid:, :] += weighs[1] + weighs[3]
        for h in range(2):
            rows_h = slice(h * mid, (h + 1) * mid)
            intra[rows_h, cols] = jnp.where(low[:mid], outs[h], outs[2 + h])
            dsc[rows_h, cols] = jnp.where(low[:mid], backs[0][h], backs[1][h])

    @pl.loop(0, pairs // 4)
    def _(k):
        prepare(4 * k + 1 - side, 0)
        prepare(4 * k + 3 - side, 1)

    carry_copy.wait_recv()

    @pl.loop(0, pairs // 4)
    def _(k):
        prepare(4 * k + side, 0)
        prepare(4 * k + 2 + side, 1)
        chain(k)

    begun = pairs // 4

    @pl.loop(0, max(pairs, own_count + LAG * (duos - 1) - begun))
    def _(i):
        chain(i + begun)

        @pl.when(i < pairs)
        def _():
            heavy(i)

    gb_acc[...] = jnp.zeros_like(gb_acc)
    gc_acc[...] = jnp.zeros_like(gc_acc)

    def project(k):
        cols = pl.ds(pl.multiple_of(k * LANES, LANES), LANES)
        gc_acc[...] += dot_nn(edy[:, cols], fin[k])
        gb_acc[...] += dot_nn(lx[:, cols], bin_[k])

    @pl.loop(0, own_count)
    def _(q):
        project(2 * q + side)

    @pl.loop(0, own_count)
    def _(q):
        k = 2 * q + 1 - side
        remote(fout.at[k], fin.at[k], f_send.at[k], f_recv.at[k], partner).wait_recv()
        remote(bout.at[k], bin_.at[k], b_send.at[k], b_recv.at[k], partner).wait_recv()
        project(k)

    top, rest = halves(dgram[...])
    grad_c = gc_acc[...] + dot_nn(top, b_mat[...]) + dot_nn(rest, b_mat[...])
    grad_b = gb_acc[...] + dot_tn(top, c_mat[...]) + dot_tn(rest, c_mat[...])
    share = rows // n_head
    whole_part[:, 0:nstate] = grad_b.astype(BF16)
    whole_part[:, nstate:] = grad_c.astype(BF16)

    def rows_of(place):
        return pl.ds(pl.multiple_of(place * share, share), share)

    def peer(off):
        return lax.rem(head + off, n_head)

    scatters, gathers = [], []
    for off in range(1, n_head):
        scatters.append(
            remote(
                whole_part.at[rows_of(peer(off))], parts.at[head],
                p_send.at[off - 1], p_recv.at[off - 1], (ctx, peer(off)),
            )
        )
        gathers.append(
            remote(
                summed.at[rows_of(head)], summed.at[rows_of(head)],
                q_send.at[off - 1], q_recv.at[off - 1], (ctx, peer(off)),
            )
        )
    for copy in scatters:
        copy.start()
    parts[head] = whole_part[rows_of(head), :]

    e_row = lax.broadcasted_iota(jnp.int32, (3 * LANES, LANES), 0)
    e_col = lax.broadcasted_iota(jnp.int32, (3 * LANES, LANES), 1)
    e_at = (e_row % LANES) // half + jnp.where(e_row < 2 * LANES, 0, heads) - e_col
    rr[...] = jnp.zeros_like(rr)

    def finish(k):
        cols = pl.ds(pl.multiple_of(k * LANES, LANES), LANES)
        st = fin[k]
        ds = bin_[k]
        skip = jnp.where(low[0:1], dskip_ref[2 * k], dskip_ref[2 * k + 1])
        step_k = step_l[:, cols]
        leave_k = leave_l[:, cols]
        xf = xc[:, cols].astype(F32)
        dyf = dy_ref[:, cols].astype(F32)
        dsc_k = dsc[:, cols]
        y_all = intra[:, cols] + enter_l[:, cols] * dot_nt(c_mat[...], st)
        y_ref[:, cols] = (y_all + skip * xf).astype(BF16)
        dlv = leave_k * dot_nt(b_mat[...], ds)
        both = dsc_k + dlv
        gp[0:rows, cols] = (step_k * both + skip * dyf) * sgrad[:, cols]
        lterm = step_k * xf * dlv
        u1 = dyf * y_all - sx[:, cols].astype(F32) * dsc_k - lterm
        top, rest = halves(u1)
        ones = jnp.where(e_at == -2 * k, 1.0, 0.0).astype(BF16)
        sums = dot_nn(jnp.concatenate([top, rest, (xf * both).astype(BF16)], axis=1), ones)
        lsum = jnp.sum(lterm, axis=0, keepdims=True)
        both_states = st.astype(F32) * ds.astype(F32) * carry_rows(carry_own, k)
        for j in range(2):
            mine = low[0:1] if j == 0 else jnp.logical_not(low[0:1])
            cs[k, j : j + 1, :] = jnp.where(mine, lsum, 0.0) + jnp.sum(
                both_states[j * half : (j + 1) * half], axis=0, keepdims=True
            )
        return sums

    @pl.loop(0, pairs // 4)
    def _(k):
        rr[...] += finish(2 * k) + finish(2 * k + 1)

    for copy in scatters:
        copy.wait_recv()
    total = parts[0].astype(F32)
    for other in range(1, n_head):
        total = total + parts[other].astype(F32)
    summed[rows_of(head), :] = total.astype(BF16)
    for copy in gathers:
        copy.start()

    @pl.loop(pairs // 4, pairs // 2)
    def _(k):
        rr[...] += finish(2 * k) + finish(2 * k + 1)

    x_rim = remote(gp.at[pl.ds(0, 8)], nxt_x, nx_send, nx_recv, before)

    @pl.when(has_prev)
    def _():
        x_rim.start()

    for copy in gathers:
        copy.wait_recv()
    gbp[0:rows, :] = summed[...].astype(F32) * sgrad_bc[...]
    bc_rim = remote(gbp.at[pl.ds(0, 8)], nxt_bc, nb_send, nb_recv, before)

    @pl.when(has_prev)
    def _():
        bc_rim.start()

    tri = jnp.where(r_id >= c_id, 1.0, 0.0)
    turned_sums = jnp.transpose(rr[...])
    extra = jnp.concatenate([cs[k, 0:2, :] for k in range(pairs)], axis=0)
    extra = jnp.sum(extra, axis=1, keepdims=True)
    d_log = exact_nn(turned_sums[:heads] + jnp.where(pos == rows - 1, extra, 0.0), tri)
    gdt_ref[...] = (turned_sums[heads : 2 * heads] - decay * d_log) * sigmoid(dt)

    @pl.when(has_next)
    def _():
        x_rim.wait_recv()

    gp[rows:, :] = nxt_x[...]

    @pl.loop(0, pairs)
    def _(k):
        cols = pl.ds(pl.multiple_of(k * LANES, LANES), LANES)
        weight = wx_ref[:, cols].astype(F32)
        total = weight[taps - 1 : taps] * gp[0:rows, cols]
        for off in range(1, taps):
            total = total + weight[taps - 1 - off : taps - off] * gp[off : off + rows, cols]
        gx_ref[:, cols] = total.astype(BF16)

    for copy in scatters + gathers:
        copy.wait_send()

    carry_copy.wait_send()

    @pl.loop(0, own_count)
    def _(q):
        k = 2 * q + side
        j = 2 * q + 1 - side
        remote(s_out.at[j], s_in.at[j], s_send.at[j], s_recv.at[j], partner).wait_send()
        remote(g_out.at[j], g_in.at[j], g_send.at[j], g_recv.at[j], partner).wait_send()
        remote(fout.at[k], fin.at[k], f_send.at[k], f_recv.at[k], partner).wait_send()
        remote(bout.at[k], bin_.at[k], b_send.at[k], b_recv.at[k], partner).wait_send()

        @pl.when(has_down)
        def _():
            remote(z_out.at[k], z_in.at[k], z_send.at[k], z_recv.at[k], z_next).wait_send()

        @pl.when(has_up)
        def _():
            remote(r_out.at[k], r_in.at[k], r_send.at[k], r_recv.at[k], z_prev).wait_send()

    @pl.when(has_next)
    def _():
        bc_rim.wait_recv()

    gbp[rows:, :] = nxt_bc[...]
    weight = wbc_ref[...].astype(F32)
    total = weight[taps - 1 : taps] * gbp[0:rows, :]
    for off in range(1, taps):
        total = total + weight[taps - 1 - off : taps - off] * gbp[off : off + rows, :]
    gbc_ref[...] = total.astype(BF16)

    @pl.when(has_prev)
    def _():
        x_rim.wait_send()
        bc_rim.wait_send()


def hand_over(*refs):
    count = len(refs) // 2
    for at in range(count):
        refs[count + at][...] = refs[at][...]


def body(n_ctx, n_head, x_raw, bc_raw, conv_x_w, conv_bc_w, dt_raw, a_log, d_skip, doc_starts, grad_y):
    rows, channels = x_raw.shape
    heads = a_log.shape[0]
    nstate = bc_raw.shape[1] // 2
    pairs = channels // LANES
    vmem = pl.BlockSpec(memory_space=pltpu.VMEM)
    smem = pl.BlockSpec(memory_space=pltpu.SMEM)
    wide = pltpu.VMEM((rows, channels), F32)
    wide_h = pltpu.VMEM((rows, channels), BF16)
    state = pltpu.VMEM((pairs, LANES, nstate), F32)
    state_h = pltpu.VMEM((pairs, LANES, nstate), BF16)
    dma = pltpu.SemaphoreType.DMA
    scratch = [
        pltpu.VMEM((RIM, channels), BF16),
        pltpu.VMEM((RIM, 2 * nstate), BF16),
        pltpu.VMEM((2, rows + 8, LANES), F32),
        pltpu.VMEM((rows + 8, 2 * nstate), F32),
        pltpu.VMEM((pairs, 8, rows), F32),
        state, state,
        pltpu.VMEM((heads, LANES), F32),
        pltpu.VMEM((heads, LANES), F32),
        state_h, state_h, state_h, state_h, state_h, state_h, state_h, state_h, state_h, state_h, state_h, state_h,
        wide_h, wide_h, wide_h, wide_h,
        wide, wide, wide, wide, wide, wide,
        pltpu.VMEM((rows + 8, channels), F32),
        pltpu.VMEM((rows + 8, 2 * nstate), F32),
        pltpu.VMEM((rows, 2 * nstate), F32),
        pltpu.VMEM((rows, nstate), BF16),
        pltpu.VMEM((rows, nstate), BF16),
        pltpu.VMEM((rows, rows), F32),
        pltpu.VMEM((rows, rows), F32),
        pltpu.VMEM((rows, rows), F32),
        pltpu.VMEM((rows, nstate), F32),
        pltpu.VMEM((rows, nstate), F32),
        pltpu.VMEM((rows, LANES), F32),
        pltpu.VMEM((pairs, 8, LANES), F32),
        pltpu.VMEM((n_head, rows // n_head, 2 * nstate), BF16),
        pltpu.VMEM((rows, 2 * nstate), BF16),
        pltpu.VMEM((rows, 2 * nstate), BF16),
        pltpu.VMEM((8, channels), F32),
        pltpu.VMEM((8, 2 * nstate), F32),
        dma, dma, dma, dma,
        dma((pairs,)), dma((pairs,)), dma((pairs,)), dma((pairs,)), dma, dma,
        dma((pairs,)), dma((pairs,)), dma((pairs,)), dma((pairs,)),
        dma((pairs,)), dma((pairs,)), dma((pairs,)), dma((pairs,)),
        dma((n_head - 1,)), dma((n_head - 1,)), dma((n_head - 1,)), dma((n_head - 1,)),
        dma, dma, dma, dma,
    ]
    shapes = (
        jax.ShapeDtypeStruct((rows, channels), BF16),
        jax.ShapeDtypeStruct((rows, channels), BF16),
        jax.ShapeDtypeStruct((rows, 2 * nstate), BF16),
        jax.ShapeDtypeStruct((heads, rows), F32),
    )
    results = pl.pallas_call(
        functools.partial(kernel, n_ctx, n_head, pairs),
        out_shape=shapes,
        in_specs=[vmem] * 5 + [smem, smem, smem, vmem],
        out_specs=(vmem, vmem, vmem, vmem),
        scratch_shapes=scratch,
        compiler_params=pltpu.CompilerParams(
            collective_id=0, has_side_effects=True, vmem_limit_bytes=56 * 1024 * 1024
        ),
        cost_estimate=pl.CostEstimate(flops=3 * 10**9, bytes_accessed=6 * 2**20, transcendentals=3 * 10**6),
    )(
        x_raw, bc_raw, conv_x_w, conv_bc_w, dt_raw, a_log, d_skip, doc_starts, grad_y
    )
    blocks = [
        pl.BlockSpec((rows // PIECES, channels), lambda i: (i, 0)),
        pl.BlockSpec((rows // PIECES, channels), lambda i: (i, 0)),
        pl.BlockSpec((rows // PIECES, 2 * nstate), lambda i: (i, 0)),
        pl.BlockSpec((heads, rows), lambda i: (0, 0)),
    ]
    return pl.pallas_call(
        hand_over, grid=(PIECES,), out_shape=shapes, in_specs=blocks, out_specs=tuple(blocks)
    )(*results)


def solution(mesh):
    in_specs = (
        P("ctx", "head"),
        P("ctx", None),
        P(None, "head"),
        P(),
        P("head", "ctx"),
        P("head"),
        P("head"),
        P("ctx"),
        P("ctx", "head"),
    )
    out_specs = (P("ctx", "head"), P("ctx", "head"), P("ctx", None), P("head", "ctx"))
    inner = functools.partial(body, mesh.shape["ctx"], mesh.shape["head"])
    return jax.shard_map(inner, mesh=mesh, in_specs=in_specs, out_specs=out_specs, check_vma=False)
```
